32 devices in a mesh: dp: 2 (over x), expert: 16 (over z, y, core).
Axes of the slice: x: 2, y: 2, z: 4, core: 2. Of those that a mesh axis runs over, the one named last changes fastest.
Arguments:
- tokens: bfloat16 [128, 5120], P(('dp', 'expert')), may hold values from -6 to 6
- chosen_expert_index: int32 [128, 6], P(('dp', 'expert')), may hold values from 0 to 15, all different within a row; in each aligned block of 4 rows (0 to 3, 4 to 7, ...) at most 3 rows name the same one
- router_gate_weight: float32 [128, 6], P(('dp', 'expert')), may hold values from 0.05 to 0.5
- partner: int32 [128], P(('dp', 'expert')), may hold values from 0 to 3, as said below
- gate_up_weight: bfloat16 [16, 2, 1536, 5120], P('expert', None, 'dp'), may hold values from -0.078125 to 0.078125
- adapter_down_weight: bfloat16 [16, 8, 1536], P('expert', None, 'dp'), may hold values from -0.15625 to 0.15625
- adapter_up_weight: bfloat16 [16, 8, 5120], P('expert', None, 'dp'), may hold values from -2 to 2
Outputs:
- down_factor_gradient: float32 [16, 8, 1536], P('expert', None, 'dp')
- up_factor_gradient: float32 [16, 8, 5120], P('expert', None, 'dp')
The draws below stay inside these ranges and needn't reach their ends.
Inputs may be any that keep to these rules, and one draw needn't show every extreme that they name: `chosen_expert_index`: in each aligned block of 4 rows (the tokens of one device) a token names 6 different experts, no expert is named by more than 3 rows, a bound that some block reaches. Tokens are paired within each aligned block of 4 rows: partner holds the index of the other token of the pair within the block, never the token itself, and partner of partner is the token.
All inputs are finite; a program needn't handle non-finite values.
Results may differ from the reference program's by a relative error of at most 0.0039.
Values may be sent and summed in bfloat16 or wider, within the bound.
No kernel may reach another device: no remote copies, remote signals or barrier semaphores. Data moves between devices by JAX's collectives and lax.ppermute only.
A program may use at most 64 MiB of HBM per device.

```python
import math
import jax
import jax.numpy as jnp
import numpy as np
from jax import lax

MODEL_WIDTH = 5120
EXPERT_UNITS = 1536
TOP = 6
ADAPTER_RANK = 8
TOK_DEV = 4
ROUTED_EXPERTS = 16
TOKENS = 128
CAP = 3


def draw_partner(key, part):
    blocks = TOKENS // TOK_DEV
    block_keys = jax.random.split(key, blocks)

    def one_block(block_key):
        order = jax.random.permutation(block_key, TOK_DEV).astype(jnp.int32)
        first = order[0::2]
        second = order[1::2]
        mates = jnp.zeros((TOK_DEV,), jnp.int32)
        mates = mates.at[first].set(second)
        return mates.at[second].set(first)
    return jax.vmap(one_block)(block_keys).reshape(TOKENS)


def level_of(key, shape, pieces, low, top_value):
    factor_of = 1.0
    for axis_at, parts in pieces:
        draws = jax.random.uniform(jax.random.fold_in(jax.random.fold_in(key, 6), axis_at), (parts,), jnp.float32, low / len(pieces), top_value / len(pieces))
        factor_of = factor_of * jnp.repeat(jnp.exp(draws), shape[axis_at] // parts).reshape((-1,) + (1,) * (len(shape) - 1 - axis_at))
    return factor_of


def assign_block(rng, own, number, rows, amount, top, bound, skew):
    ranking = jax.random.permutation(rng, amount)
    packed, common = shares(amount, rows * top, bound, skew, True), shares(amount, rows * top, bound, skew, False)
    places = jnp.arange(amount)

    def named(lengths, turn):
        used = int((lengths > 0).sum())
        fixed = max(1, used // 4)
        shifted = fixed + (places - fixed + turn * (used - fixed)) % max(1, amount - fixed)
        return jnp.zeros((amount,), jnp.int32).at[ranking[jnp.where(places < fixed, places, shifted)]].set(jnp.asarray(lengths, jnp.int32))

    lengths = jnp.where(number % 4 == 0, named(packed, number // 4), named(common, number - number // 4 - 1))
    mixed = jax.random.permutation(jax.random.fold_in(own, 3), amount)
    donor, receiver = mixed[0:amount // 2 * 2:2], mixed[1:amount // 2 * 2:2]
    slack = jnp.minimum(lengths[donor] - 1, bound - lengths[receiver]) // 2
    slack = jnp.where((donor == ranking[0]) | (receiver == ranking[0]) | (lengths[receiver] == 0), 0, jnp.maximum(slack, 0))
    shifted = jax.random.randint(jax.random.fold_in(own, 4), (amount // 2,), 0, 1 << 20) % (slack + 1)
    lengths = lengths.at[donor].add(-shifted).at[receiver].add(shifted)
    items = jnp.searchsorted(jnp.cumsum(lengths), jnp.arange(rows * top), side="right").astype(jnp.int32)
    grid = items.reshape(top, rows).T
    grid = grid[jax.random.permutation(jax.random.fold_in(own, 1), rows)]
    turn = jax.random.randint(jax.random.fold_in(own, 2), (rows, 1), 0, top)
    return jnp.take_along_axis(grid, (jnp.arange(top)[None, :] + turn) % top, axis=1)


def shares(number_of, total, limit, lean, full):
    loads = [(1 << 20) // math.isqrt(rank ** lean) + 1 for rank in range(1, number_of + 1)]
    largest = limit if full else min(limit, max(-(-total // number_of), total * loads[0] // sum(loads)))
    least = 1 if total - largest >= number_of - 1 else 0
    counts, spare = [largest] + [least] * (number_of - 1), total - largest - least * (number_of - 1)
    while spare > 0:
        free = [i for i in range(1, number_of) if counts[i] < largest] or [i for i in range(1, number_of) if counts[i] < limit]
        whole, left = sum([loads[i] for i in free]), spare
        for i in free:
            addition = min(limit - counts[i], max(1, left * loads[i] // whole), spare)
            counts[i] = counts[i] + addition
            spare = spare - addition
    return np.array(counts)


def bell_draw(own_key, extent, spread, bound, pieces=(), kind=jnp.bfloat16):
    drawn = jax.random.normal(own_key, extent, jnp.float32) * spread
    if len(pieces) > 0:
        drawn = level_of(own_key, extent, pieces, -0.22, 0.18) * drawn
    return jnp.clip(drawn, min=-bound, max=bound).astype(kind)


def setup_inputs(seed: int = 0) -> dict:
    arg_keys = jax.random.split(jax.random.key(seed), 8)
    tokens = bell_draw(arg_keys[0], (TOKENS, MODEL_WIDTH), 1.0, 6.0, ((0, 32),))
    chosen_expert_index_keys = jax.random.split(jax.random.fold_in(arg_keys[1], 1), TOKENS // TOK_DEV)
    chosen_expert_index_turns = jax.random.permutation(jax.random.fold_in(arg_keys[1], 3), TOKENS // TOK_DEV)
    chosen_expert_index = jax.vmap(lambda own, number: assign_block(jax.random.fold_in(arg_keys[1], 2), own, number, TOK_DEV, ROUTED_EXPERTS, TOP, CAP, 2))(chosen_expert_index_keys, chosen_expert_index_turns).reshape((TOKENS, TOP))
    router_gate_weight = jnp.clip(0.05 + 0.45 * jax.random.uniform(arg_keys[2], (TOKENS, TOP), jnp.float32) ** level_of(arg_keys[2], (TOKENS, TOP), ((0, 32),), -0.2, 0.2), 0.05, 0.5)
    partner = draw_partner(jax.random.fold_in(arg_keys[7], 71), 0)
    gate_up_weight = bell_draw(arg_keys[4], (ROUTED_EXPERTS, 2, EXPERT_UNITS, MODEL_WIDTH), MODEL_WIDTH ** -0.5, 0.078125, ((0, 16), (2, 2)))
    adapter_down_weight = bell_draw(arg_keys[5], (ROUTED_EXPERTS, ADAPTER_RANK, EXPERT_UNITS), EXPERT_UNITS ** -0.5, 0.15625, ((0, 16), (2, 2)))
    adapter_up_weight = bell_draw(arg_keys[6], (ROUTED_EXPERTS, ADAPTER_RANK, MODEL_WIDTH), ADAPTER_RANK ** -0.5, 2.0, ((0, 16), (2, 2)))
    return {"tokens": tokens, "chosen_expert_index": chosen_expert_index, "router_gate_weight": router_gate_weight, "partner": partner, "gate_up_weight": gate_up_weight, "adapter_down_weight": adapter_down_weight, "adapter_up_weight": adapter_up_weight}


adapter_scale = 2.0
control = 0.5
highest_precision = lax.Precision.HIGHEST

def reference(tokens, chosen_expert_index, router_gate_weight, partner, gate_up_weight, adapter_down_weight, adapter_up_weight):
    blocks = TOKENS // TOK_DEV
    x_blocks = tokens.reshape(blocks, TOK_DEV, MODEL_WIDTH)
    x_wide = x_blocks.astype(jnp.float32)
    ids = chosen_expert_index.reshape(blocks, TOK_DEV, TOP)
    weights = router_gate_weight.reshape(blocks, TOK_DEV, TOP)
    picks = (ids[..., None] == jnp.arange(ROUTED_EXPERTS, dtype=jnp.int32)).astype(jnp.int32)
    flat = picks.reshape(blocks, TOK_DEV * TOP, ROUTED_EXPERTS)
    before = jnp.cumsum(flat, axis=1) - flat
    slots = lax.optimization_barrier(jnp.sum(before * flat, axis=2)).reshape(blocks, TOK_DEV, TOP)
    places = (slots[..., None] == jnp.arange(CAP, dtype=jnp.int32)).astype(jnp.float32)

    def tables(expert_number):
        chosen = (ids == expert_number).astype(jnp.float32)
        select = jnp.einsum('btk,btkc->bct', chosen, places, precision=highest_precision)
        weighted = jnp.einsum('btk,btkc,btk->bct', chosen, places, weights, precision=highest_precision)
        return (select, weighted)

    def forward(carry, expert_number):
        select, weighted = tables(expert_number)
        rows = jnp.einsum('bct,btd->bcd', select, x_wide, precision=highest_precision).astype(jnp.bfloat16)
        weight = lax.dynamic_index_in_dim(gate_up_weight, expert_number, 0, keepdims=False).astype(jnp.float32)
        both = jnp.einsum('bcd,gfd->bcgf', rows.astype(jnp.float32), weight, precision=highest_precision)
        hidden_state = (jax.nn.silu(both[:, :, 0]) * both[:, :, 1]).astype(jnp.bfloat16)
        down_factor = lax.dynamic_index_in_dim(adapter_down_weight, expert_number, 0, keepdims=False).astype(jnp.float32)
        up_factor = lax.dynamic_index_in_dim(adapter_up_weight, expert_number, 0, keepdims=False).astype(jnp.float32)
        narrow_product = jnp.einsum('bcf,rf->bcr', hidden_state.astype(jnp.float32), down_factor, precision=highest_precision)
        change_rows = (adapter_scale * jnp.einsum('gxl,lz->gxz', narrow_product, up_factor, precision=highest_precision)).astype(jnp.bfloat16)
        carry = carry + jnp.einsum('bct,bcd->btd', weighted, change_rows.astype(jnp.float32), precision=highest_precision)
        return (carry, (hidden_state, narrow_product))
    expert_range = jnp.arange(ROUTED_EXPERTS, dtype=jnp.int32)
    start = jnp.zeros((blocks, TOK_DEV, MODEL_WIDTH), jnp.float32)
    delta, (hiddens, lows) = lax.scan(forward, start, expert_range)
    mates = jnp.take_along_axis(x_blocks, partner.reshape(blocks, TOK_DEV)[..., None].astype(jnp.int32), axis=1)
    direction = x_wide - mates.astype(jnp.float32)
    cotangent = 2.0 / math.sqrt(TOKENS) * (delta - control * direction)

    def backward(pack):
        expert_number, hidden_state, narrow_product = pack
        select, weighted = tables(expert_number)
        cot_rows = jnp.einsum('bct,btd->bcd', weighted, cotangent, precision=highest_precision).astype(jnp.bfloat16)
        up_factor = lax.dynamic_index_in_dim(adapter_up_weight, expert_number, 0, keepdims=False).astype(jnp.float32)
        cotangent_broad = cot_rows.astype(jnp.float32)
        cotangent_narrow = jnp.einsum('bcd,rd->bcr', cotangent_broad, up_factor, precision=highest_precision)
        up_factor_gradient = adapter_scale * jnp.einsum('wsv,wsg->vg', narrow_product, cotangent_broad, precision=highest_precision)
        down_factor_gradient = adapter_scale * jnp.einsum('mpi,mpq->iq', cotangent_narrow, hidden_state.astype(jnp.float32), precision=highest_precision)
        return (down_factor_gradient, up_factor_gradient)
    down_factor_gradient, up_factor_gradient = lax.map(backward, (expert_range, hiddens, lows))
    return (down_factor_gradient, up_factor_gradient)
```

```python
import functools
import math

import jax
import jax.numpy as jnp
from jax import lax
from jax.experimental import pallas as pl
from jax.experimental.pallas import tpu as pltpu
from jax.sharding import Mesh
from jax.sharding import PartitionSpec as P

adapter_scale = 2.0
control = 0.5
highest_precision = lax.Precision.HIGHEST
f32 = jnp.float32
bf16 = jnp.bfloat16
every = ("dp", "chip", "core")
mib = 1 << 20


def route_tables(chosen_expert_index, router_gate_weight, experts, capacity):
    tok_count, choices = chosen_expert_index.shape
    picks = (chosen_expert_index[:, :, None] == jnp.arange(experts, dtype=jnp.int32)).astype(
        jnp.int32
    )
    flat = picks.reshape(tok_count * choices, experts)
    before = jnp.cumsum(flat, axis=0) - flat
    slots = jnp.sum(before * flat, axis=1).reshape(tok_count, choices)
    places = (slots[:, :, None] == jnp.arange(capacity, dtype=jnp.int32)).astype(jnp.float32)
    chosen = picks.astype(jnp.float32)
    select = jnp.einsum("tke,tkc->ect", chosen, places, precision=highest_precision)
    weighted = jnp.einsum(
        "tke,tkc,tk->ect", chosen, places, router_gate_weight, precision=highest_precision
    )
    return (select.astype(jnp.bfloat16), weighted)


def expert_hidden(rows, w_local):
    flat_rows = rows.reshape(-1, rows.shape[-1])
    both = jnp.einsum("gfd,nd->gfn", w_local, flat_rows, preferred_element_type=jnp.float32)
    return (jax.nn.silu(both[0]) * both[1]).astype(jnp.bfloat16)


def slot_body(
    tokens,
    chosen_expert_index,
    router_gate_weight,
    partner,
    gate_up_weight,
    adapter_down_weight,
    adapter_up_weight,
):
    tok_count, width = tokens.shape
    choices = chosen_expert_index.shape[1]
    groups = lax.axis_size("dp")
    experts = lax.axis_size("expert")
    capacity = min(tok_count, max(2, (2 * tok_count * choices + experts - 1) // experts))
    select, weighted = route_tables(chosen_expert_index, router_gate_weight, experts, capacity)
    w_local = gate_up_weight[0]
    down_factor = adapter_down_weight[0]
    up_factor = adapter_up_weight[0]
    slice_width = up_factor.shape[1]
    outgoing = jnp.einsum("ect,td->ecd", select, tokens, preferred_element_type=jnp.float32).astype(
        jnp.bfloat16
    )
    arrived = lax.all_to_all(outgoing[None], "expert", split_axis=1, concat_axis=1, tiled=True)
    hidden_state = expert_hidden(lax.all_gather(arrived, "dp", axis=0, tiled=True), w_local)
    grid = (groups, experts, capacity)
    partial_low = jnp.einsum(
        "fn,rf->nr", hidden_state, down_factor, preferred_element_type=jnp.float32
    )
    narrow_product = lax.psum(partial_low, "dp")
    delta_flat = (
        adapter_scale
        * jnp.einsum(
            "hy,ya->ha", narrow_product, up_factor.astype(jnp.float32), precision=highest_precision
        )
    ).astype(jnp.bfloat16)
    change_rows = delta_flat.reshape(grid + (slice_width,))
    returned = lax.all_to_all(
        lax.all_to_all(change_rows, "dp", split_axis=0, concat_axis=3, tiled=True),
        "expert",
        split_axis=1,
        concat_axis=1,
        tiled=True,
    )
    returned = returned.reshape(experts, capacity, width)
    delta = jnp.einsum(
        "ect,ecd->td", weighted, returned.astype(jnp.float32), precision=highest_precision
    )
    total = tok_count * groups * experts
    mates = jnp.take(tokens, partner, axis=0).astype(jnp.float32)
    direction = tokens.astype(jnp.float32) - mates
    cotangent = 2.0 / math.sqrt(total) * (delta - control * direction)
    cot_rows = jnp.einsum("ect,td->ecd", weighted, cotangent, precision=highest_precision).astype(
        jnp.bfloat16
    )
    sectioned = cot_rows.reshape(1, experts, capacity, groups, slice_width)
    cot_in = lax.all_to_all(
        lax.all_to_all(sectioned, "dp", split_axis=3, concat_axis=0, tiled=True),
        "expert",
        split_axis=1,
        concat_axis=1,
        tiled=True,
    )
    cot_in = cot_in.reshape(-1, slice_width)
    partial_cot = jnp.einsum("nd,rd->nr", cot_in, up_factor, preferred_element_type=jnp.float32)
    cotangent_narrow = lax.psum(partial_cot, "dp")
    up_factor_gradient = adapter_scale * jnp.einsum(
        "nr,nd->rd", narrow_product, cot_in.astype(jnp.float32), precision=highest_precision
    )
    down_factor_gradient = adapter_scale * jnp.einsum(
        "nr,fn->rf", cotangent_narrow, hidden_state.astype(jnp.float32), precision=highest_precision
    )
    return (down_factor_gradient[None], up_factor_gradient[None])


def mask_of(block):
    return (
        ((block & 1) << 2)
        | (((block >> 1) & 1) << 3)
        | (((block >> 2) & 1) << 4)
        | (((block >> 3) & 1) << 1)
        | ((block >> 4) & 1)
    )


def own_number():
    return (lax.axis_index("dp") * lax.axis_size("chip") + lax.axis_index("chip")) * 2 + (
        lax.axis_index("core")
    )


def dot(left, right, left_dim, right_dim, precision=None):
    return lax.dot_general(
        left,
        right,
        (((left_dim,), (right_dim,)), ((), ())),
        precision=precision,
        preferred_element_type=f32,
    )


def split_two(value):
    high = value.astype(bf16)
    return high, (value - high.astype(f32)).astype(bf16)


def order_table(count):
    lane = lax.broadcasted_iota(jnp.int32, (count, count), 1)
    row = lax.broadcasted_iota(jnp.int32, (count, count), 0)
    whole = ((mask_of(lane >> 2) ^ own_number()) << 2) | (lane & 3)
    return (row == whole).astype(f32).astype(bf16)


def meta_kernel(index_ref, gate_ref, partner_ref, meta_ref, index_s, gate_s, partner_s, sems):
    copies = [
        pltpu.make_async_copy(index_ref, index_s, sems.at[0]),
        pltpu.make_async_copy(gate_ref, gate_s, sems.at[1]),
        pltpu.make_async_copy(partner_ref, partner_s, sems.at[2]),
    ]
    for copy in copies:
        copy.start()
    for copy in copies:
        copy.wait()
    lane = lax.broadcasted_iota(jnp.int32, (8, 128), 1)
    row = lax.broadcasted_iota(jnp.int32, (8, 128), 0)
    dense = jnp.zeros((8, 128), f32)
    mates = jnp.zeros((8, 128), f32)
    for t in range(index_ref.shape[0]):
        for k in range(index_ref.shape[1]):
            dense = dense + jnp.where((lane & 63) == index_s[t, k] * 4 + t, gate_s[t, k], 0.0)
        mates = mates + jnp.where(lane == 64 + t, partner_s[t].astype(f32), 0.0)
    high = dense.astype(bf16).astype(f32)
    middle = (dense - high).astype(bf16).astype(f32)
    low = dense - high - middle
    first = jnp.where(lane < 64, high, middle)
    second = jnp.where(lane < 64, low, mates)
    rows = jnp.where(row == 0, first, jnp.where(row == 1, second, 0.0))
    meta_ref[...] = jnp.concatenate([jnp.zeros((8, 128), f32), rows], axis=0).astype(bf16)


def whole_rows_kernel(own_ref, other_ref, out_ref):
    half = own_ref.shape[1]
    at = pl.multiple_of(lax.axis_index("dp") * half, 128)
    out_ref[:, pl.ds(at, half)] = own_ref[...]
    at = pl.multiple_of((1 - lax.axis_index("dp")) * half, 128)
    out_ref[:, pl.ds(at, half)] = other_ref[...]


def hidden_kernel(chunks, pieces, *refs):
    x_refs = refs[:pieces]
    w_ref, v_ref, up_ref, meta_ref = refs[pieces : pieces + 4]
    hid_ref, low_ref, cross_ref, send_ref = refs[pieces + 4 : pieces + 8]
    x_all, w_buf, sems = refs[pieces + 8 :]
    units = w_ref.shape[1]
    step = units // chunks

    def fetch(i):
        return pltpu.make_async_copy(w_ref.at[:, pl.ds(i * step, step), :], w_buf.at[i], sems.at[i])

    ahead = 3
    for i in range(ahead):
        fetch(i).start()
    rows = x_refs[0].shape[0]
    for p in range(pieces):
        x_all[pl.ds(p * rows, rows), :] = x_refs[p][...]
    x = x_all[...]
    low = jnp.zeros(low_ref.shape, f32)
    for i in range(chunks):
        fetch(i).wait()
        if i + ahead < chunks:
            fetch(i + ahead).start()
        gate = dot(w_buf[i, 0], x, 1, 1)
        up = dot(w_buf[i, 1], x, 1, 1)
        hidden = (gate / (1.0 + jnp.exp(-gate)) * up).astype(bf16)
        hid_ref[pl.ds(i * step, step), :] = hidden
        low = low + dot(v_ref[:, pl.ds(i * step, step)], hidden, 1, 0)
    low_ref[...] = low
    cross_ref[...] = dot(up_ref[...], x, 1, 1)
    ordered = dot(low.astype(bf16), order_table(x.shape[0]), 1, 1)
    block = jnp.concatenate([ordered, jnp.zeros_like(ordered)], axis=0).astype(bf16)
    block = block + meta_ref[...]
    for i in range(send_ref.shape[0]):
        send_ref[i] = block


def gradient_kernel(pieces, *refs):
    x_refs = refs[:pieces]
    near_ref, far_ref, up_near, up_far, hid_ref, low_ref, cross_ref = refs[pieces : pieces + 7]
    down_out, up_out = refs[pieces + 7 : pieces + 9]
    blocks_buf, wide_buf = refs[pieces + 9 :]
    tokens = hid_ref.shape[1]
    blocks = tokens // 4
    half = up_out.shape[1]
    dp = lax.axis_index("dp")
    chip = lax.axis_index("chip")
    chips = lax.axis_size("chip")
    at = pl.multiple_of(dp * half, 128)
    for b in range(blocks):
        mask = mask_of(b)
        source = far_ref if mask & 1 else near_ref
        blocks_buf[b] = source[(dp ^ (mask >> 4)) * chips + (chip ^ ((mask >> 1) & 7))]
    received = blocks_buf[...]
    local = dot(received.reshape(blocks * 16, tokens), order_table(tokens), 1, 0)
    local = local.reshape(4, 2, 4, 16, tokens)[:, :, :, 0:8]
    lows = (local[:, 0] + local[:, 1]).reshape(16, 8, tokens)
    own_low = low_ref[...] + local[0, 1, 0]

    lane = lax.broadcasted_iota(jnp.int32, (blocks, tokens), 1)
    row = lax.broadcasted_iota(jnp.int32, (blocks, tokens), 0)
    spread = ((lane >> 2) == row).astype(f32).astype(bf16)
    wide = received.astype(f32)
    first = dot(wide[:, 8].astype(bf16), spread, 0, 0)
    second = dot(wide[:, 9].astype(bf16), spread, 0, 0)
    lane = lax.broadcasted_iota(jnp.int32, (tokens, tokens), 1)
    row = lax.broadcasted_iota(jnp.int32, (tokens, tokens), 0)
    same = (row & 3) == (lane & 3)
    first = jnp.where(same, first, 0.0)
    second = jnp.where(same, second, 0.0)
    mate = jnp.sum(second[64:72], axis=0, keepdims=True).astype(jnp.int32)
    mate = (lax.broadcasted_iota(jnp.int32, (1, tokens), 1) & ~3) | mate
    k = row >> 3
    away = ((k & 1) << 2) | (((k >> 1) & 1) << 3) | (((k >> 2) & 1) << 1) | ((k >> 3) & 1)
    expert = (own_number() & 15) ^ away
    pick = ((lane >> 2) & 15) == expert
    pick_first = pick.astype(f32).astype(bf16)
    pick_second = (pick & (lane < 64)).astype(f32).astype(bf16)
    gates = dot(pick_first, first.astype(bf16), 1, 0) + dot(pick_second, second.astype(bf16), 1, 0)

    scale = 2.0 / math.sqrt(tokens)
    weight = scale * gates[0:1]
    upper = adapter_scale * gates * lows.reshape(tokens, tokens) * weight
    apart = (row == lane).astype(f32) - (row == mate).astype(f32)
    lower = -control * apart * weight
    factors = jnp.concatenate([upper, lower], axis=0)

    whole_up = jnp.concatenate([up_near[...], up_far[...]], axis=0)
    gram = dot(up_near[0:8, :], whole_up, 1, 1)
    products = jnp.concatenate([gram, cross_ref[...]], axis=1)
    cot_low = dot(products, factors, 1, 0, highest_precision)
    high, low = split_two(adapter_scale * cot_low)
    down = dot(jnp.concatenate([high, low], axis=0), hid_ref[...], 1, 1)
    down_out[...] = down[0:8] + down[8:16]

    rows = x_refs[0].shape[0]
    near_rows = up_near.shape[0]
    wide_buf[pl.ds(0, near_rows), :] = up_near[:, pl.ds(at, half)]
    wide_buf[pl.ds(near_rows, near_rows), :] = up_far[:, pl.ds(at, half)]
    for p in range(pieces):
        wide_buf[pl.ds(2 * near_rows + p * rows, rows), :] = x_refs[p][:, pl.ds(at, half)]
    mixed = dot(own_low, factors, 1, 1, highest_precision)
    high, low = split_two(adapter_scale * mixed)
    up = dot(jnp.concatenate([high, low], axis=0), wide_buf[...], 1, 0)
    up_out[...] = up[0:8] + up[8:16]


def dense_body(
    tokens,
    chosen_expert_index,
    router_gate_weight,
    partner,
    gate_up_weight,
    adapter_down_weight,
    adapter_up_weight,
):
    tok_count, width = tokens.shape
    devices = lax.axis_size("dp") * lax.axis_size("chip") * lax.axis_size("core")
    total = tok_count * devices
    units = gate_up_weight.shape[2]
    rank = adapter_up_weight.shape[1]
    half = adapter_up_weight.shape[2]
    vmem = pl.BlockSpec(memory_space=pltpu.VMEM)
    anywhere = pl.BlockSpec(memory_space=pl.ANY)

    def swap(value, mask):
        return lax.ppermute(value, every, [(i, i ^ mask) for i in range(devices)])

    def grow(value, mask):
        return jnp.concatenate([value, swap(value, mask)], axis=0)

    meta = pl.pallas_call(
        meta_kernel,
        out_shape=jax.ShapeDtypeStruct((16, total), bf16),
        in_specs=[anywhere] * 3,
        out_specs=vmem,
        scratch_shapes=[
            pltpu.SMEM(chosen_expert_index.shape, jnp.int32),
            pltpu.SMEM(router_gate_weight.shape, f32),
            pltpu.SMEM(partner.shape, jnp.int32),
            pltpu.SemaphoreType.DMA((3,)),
        ],
        name="meta",
    )(chosen_expert_index, router_gate_weight, partner)

    column = grow(grow(tokens, 4), 8)
    near = [column, swap(column, 16), swap(column, 2), swap(column, 18)]
    pieces = near + [swap(piece, 1) for piece in near]

    own_up = adapter_up_weight[0]
    whole_up = pl.pallas_call(
        whole_rows_kernel,
        out_shape=jax.ShapeDtypeStruct((rank, width), bf16),
        in_specs=[vmem, vmem],
        out_specs=vmem,
        name="whole_rows",
    )(own_up, swap(own_up, 16))
    up_near = grow(grow(grow(whole_up, 4), 8), 2)
    up_far = swap(up_near, 1)

    chunks = 6
    count = len(pieces)
    hidden, low, cross, send = pl.pallas_call(
        functools.partial(hidden_kernel, chunks, count),
        out_shape=(
            jax.ShapeDtypeStruct((units, total), bf16),
            jax.ShapeDtypeStruct((rank, total), f32),
            jax.ShapeDtypeStruct((rank, total), f32),
            jax.ShapeDtypeStruct((devices // 2, 16, total), bf16),
        ),
        in_specs=[vmem] * count + [anywhere] + [vmem] * 3,
        out_specs=(vmem,) * 4,
        scratch_shapes=[
            pltpu.VMEM((total, width), bf16),
            pltpu.VMEM((chunks, 2, units // chunks, width), bf16),
            pltpu.SemaphoreType.DMA((chunks,)),
        ],
        compiler_params=pltpu.CompilerParams(vmem_limit_bytes=40 * mib),
        name="hidden",
    )(*pieces, gate_up_weight[0], adapter_down_weight[0], whole_up, meta)

    from_near = lax.all_to_all(send, ("dp", "chip"), split_axis=0, concat_axis=0, tiled=True)
    from_far = swap(from_near, 1)

    down, up = pl.pallas_call(
        functools.partial(gradient_kernel, count),
        out_shape=(
            jax.ShapeDtypeStruct((rank, units), f32),
            jax.ShapeDtypeStruct((rank, half), f32),
        ),
        in_specs=[vmem] * (count + 7),
        out_specs=(vmem, vmem),
        scratch_shapes=[
            pltpu.VMEM((devices, 16, total), bf16),
            pltpu.VMEM((2 * total, half), bf16),
        ],
        compiler_params=pltpu.CompilerParams(vmem_limit_bytes=32 * mib),
        name="gradient",
    )(*pieces, from_near, from_far, up_near, up_far, hidden, low, cross)
    return (down[None], up[None])


def solution(mesh):
    groups, experts = mesh.shape["dp"], mesh.shape["expert"]
    if (groups, experts) == (2, 16):
        cut = Mesh(mesh.devices.reshape(groups, experts // 2, 2), every)
        data, owners = every, ("chip", "core")
        run, mesh = dense_body, cut
    else:
        data, owners = ("dp", "expert"), "expert"
        run = slot_body
    placed = (
        P(data, None),
        P(data, None),
        P(data, None),
        P(data),
        P(owners, None, "dp", None),
        P(owners, None, "dp"),
        P(owners, None, "dp"),
    )
    return jax.shard_map(
        run,
        mesh=mesh,
        in_specs=placed,
        out_specs=(P(owners, None, "dp"), P(owners, None, "dp")),
        check_vma=False,
    )
```

```python
import functools
import math

import jax
import jax.numpy as jnp
from jax import lax
from jax.experimental import pallas as pl
from jax.experimental.pallas import tpu as pltpu
from jax.sharding import Mesh
from jax.sharding import PartitionSpec as P

adapter_scale = 2.0
control = 0.5
highest_precision = lax.Precision.HIGHEST
f32 = jnp.float32
bf16 = jnp.bfloat16
every = ("dp", "chip", "core")
mib = 1 << 20


def route_tables(chosen_expert_index, router_gate_weight, experts, capacity):
    tok_count, choices = chosen_expert_index.shape
    picks = (chosen_expert_index[:, :, None] == jnp.arange(experts, dtype=jnp.int32)).astype(
        jnp.int32
    )
    flat = picks.reshape(tok_count * choices, experts)
    before = jnp.cumsum(flat, axis=0) - flat
    slots = jnp.sum(before * flat, axis=1).reshape(tok_count, choices)
    places = (slots[:, :, None] == jnp.arange(capacity, dtype=jnp.int32)).astype(jnp.float32)
    chosen = picks.astype(jnp.float32)
    select = jnp.einsum("tke,tkc->ect", chosen, places, precision=highest_precision)
    weighted = jnp.einsum(
        "tke,tkc,tk->ect", chosen, places, router_gate_weight, precision=highest_precision
    )
    return (select.astype(jnp.bfloat16), weighted)


def expert_hidden(rows, w_local):
    flat_rows = rows.reshape(-1, rows.shape[-1])
    both = jnp.einsum("gfd,nd->gfn", w_local, flat_rows, preferred_element_type=jnp.float32)
    return (jax.nn.silu(both[0]) * both[1]).astype(jnp.bfloat16)


def slot_body(
    tokens,
    chosen_expert_index,
    router_gate_weight,
    partner,
    gate_up_weight,
    adapter_down_weight,
    adapter_up_weight,
):
    tok_count, width = tokens.shape
    choices = chosen_expert_index.shape[1]
    groups = lax.axis_size("dp")
    experts = lax.axis_size("expert")
    capacity = min(tok_count, max(2, (2 * tok_count * choices + experts - 1) // experts))
    select, weighted = route_tables(chosen_expert_index, router_gate_weight, experts, capacity)
    w_local = gate_up_weight[0]
    down_factor = adapter_down_weight[0]
    up_factor = adapter_up_weight[0]
    slice_width = up_factor.shape[1]
    outgoing = jnp.einsum("ect,td->ecd", select, tokens, preferred_element_type=jnp.float32).astype(
        jnp.bfloat16
    )
    arrived = lax.all_to_all(outgoing[None], "expert", split_axis=1, concat_axis=1, tiled=True)
    hidden_state = expert_hidden(lax.all_gather(arrived, "dp", axis=0, tiled=True), w_local)
    grid = (groups, experts, capacity)
    partial_low = jnp.einsum(
        "fn,rf->nr", hidden_state, down_factor, preferred_element_type=jnp.float32
    )
    narrow_product = lax.psum(partial_low, "dp")
    delta_flat = (
        adapter_scale
        * jnp.einsum(
            "hy,ya->ha", narrow_product, up_factor.astype(jnp.float32), precision=highest_precision
        )
    ).astype(jnp.bfloat16)
    change_rows = delta_flat.reshape(grid + (slice_width,))
    returned = lax.all_to_all(
        lax.all_to_all(change_rows, "dp", split_axis=0, concat_axis=3, tiled=True),
        "expert",
        split_axis=1,
        concat_axis=1,
        tiled=True,
    )
    returned = returned.reshape(experts, capacity, width)
    delta = jnp.einsum(
        "ect,ecd->td", weighted, returned.astype(jnp.float32), precision=highest_precision
    )
    total = tok_count * groups * experts
    mates = jnp.take(tokens, partner, axis=0).astype(jnp.float32)
    direction = tokens.astype(jnp.float32) - mates
    cotangent = 2.0 / math.sqrt(total) * (delta - control * direction)
    cot_rows = jnp.einsum("ect,td->ecd", weighted, cotangent, precision=highest_precision).astype(
        jnp.bfloat16
    )
    sectioned = cot_rows.reshape(1, experts, capacity, groups, slice_width)
    cot_in = lax.all_to_all(
        lax.all_to_all(sectioned, "dp", split_axis=3, concat_axis=0, tiled=True),
        "expert",
        split_axis=1,
        concat_axis=1,
        tiled=True,
    )
    cot_in = cot_in.reshape(-1, slice_width)
    partial_cot = jnp.einsum("nd,rd->nr", cot_in, up_factor, preferred_element_type=jnp.float32)
    cotangent_narrow = lax.psum(partial_cot, "dp")
    up_factor_gradient = adapter_scale * jnp.einsum(
        "nr,nd->rd", narrow_product, cot_in.astype(jnp.float32), precision=highest_precision
    )
    down_factor_gradient = adapter_scale * jnp.einsum(
        "nr,fn->rf", cotangent_narrow, hidden_state.astype(jnp.float32), precision=highest_precision
    )
    return (down_factor_gradient[None], up_factor_gradient[None])


def mask_of(block):
    return (
        ((block & 1) << 3)
        | (((block >> 1) & 1) << 2)
        | (((block >> 2) & 1) << 4)
        | (((block >> 3) & 1) << 1)
        | ((block >> 4) & 1)
    )


def own_number():
    return (lax.axis_index("dp") * lax.axis_size("chip") + lax.axis_index("chip")) * 2 + (
        lax.axis_index("core")
    )


def dot(left, right, left_dim, right_dim, precision=None):
    return lax.dot_general(
        left,
        right,
        (((left_dim,), (right_dim,)), ((), ())),
        precision=precision,
        preferred_element_type=f32,
    )


def split_two(value):
    high = value.astype(bf16)
    return high, (value - high.astype(f32)).astype(bf16)


def order_table(count):
    lane = lax.broadcasted_iota(jnp.int32, (count, count), 1)
    row = lax.broadcasted_iota(jnp.int32, (count, count), 0)
    whole = ((mask_of(lane >> 2) ^ own_number()) << 2) | (lane & 3)
    return (row == whole).astype(f32).astype(bf16)


def start_kernel(
    x_ref, u_ref, index_ref, gate_ref, partner_ref, out_ref, up_ref, index_v, gate_v, partner_s, sems
):
    count, width = x_ref.shape
    copies = [
        pltpu.make_async_copy(index_ref, index_v, sems.at[0]),
        pltpu.make_async_copy(gate_ref, gate_v, sems.at[1]),
        pltpu.make_async_copy(partner_ref, partner_s, sems.at[2]),
        pltpu.make_async_copy(u_ref, up_ref, sems.at[3]),
        pltpu.make_async_copy(x_ref, out_ref.at[:, pl.ds(0, width)], sems.at[4]),
    ]
    for copy in copies:
        copy.start()
    for copy in copies[:3]:
        copy.wait()
    lane = lax.broadcasted_iota(jnp.int32, (count, 128), 1)
    row = lax.broadcasted_iota(jnp.int32, (count, 128), 0)
    index, gate = index_v[...], gate_v[...]
    dense = jnp.zeros((count, 128), f32)
    for k in range(index.shape[1]):
        dense = dense + jnp.where((lane & 15) == index[:, k : k + 1], gate[:, k : k + 1], 0.0)
    mates = jnp.zeros((count, 128), f32)
    for t in range(count):
        mates = mates + jnp.where((row == t) & (lane == 48), partner_s[t].astype(f32), 0.0)
    high = dense.astype(bf16).astype(f32)
    middle = (dense - high).astype(bf16).astype(f32)
    low = dense - high - middle
    parts = jnp.where(lane < 16, high, jnp.where(lane < 32, middle, jnp.where(lane < 48, low, mates)))
    out_ref[:, pl.ds(width, 128)] = parts.astype(bf16)
    copies[3].wait()
    copies[4].wait()


def fetch_kernel(first, w_ref, v_ref, w_out, v_out, sems):
    units = w_out.shape[1]
    parts = sems.shape[0] - 1
    rows = units // parts
    copies = [pltpu.make_async_copy(v_ref.at[:, pl.ds(first, units)], v_out, sems.at[parts])]
    for i in range(parts):
        copies.append(
            pltpu.make_async_copy(
                w_ref.at[:, pl.ds(first + i * rows, rows), :], w_out.at[:, pl.ds(i * rows, rows), :], sems.at[i]
            )
        )
    for copy in copies:
        copy.start()
    for copy in copies:
        copy.wait()


def join_kernel(first_ref, second_ref, out_ref):
    rows = first_ref.shape[0]
    out_ref[pl.ds(0, rows), :] = first_ref[...]
    out_ref[pl.ds(rows, rows), :] = second_ref[...]


def hidden_kernel(step, pieces, *refs):
    x_refs = refs[:pieces]
    early_w, early_v, late_w, late_v, own_up, other_up = refs[pieces : pieces + 6]
    hid_ref, low_ref, cross_ref, gate_ref, x_all = refs[pieces + 6 :]
    at = 0
    for ref in x_refs:
        x_all[pl.ds(at, ref.shape[0]), :] = ref[...]
        at += ref.shape[0]
    width = early_w.shape[2]
    half = width // 2
    x = x_all[:, pl.ds(0, width)]
    low = jnp.zeros(low_ref.shape, f32)
    base = 0
    for w_ref, v_ref in ((early_w, early_v), (late_w, late_v)):
        for at in range(0, w_ref.shape[1], step):
            gate = dot(w_ref[0, pl.ds(at, step), :], x, 1, 1)
            up = dot(w_ref[1, pl.ds(at, step), :], x, 1, 1)
            hidden = (gate / (1.0 + jnp.exp(-gate)) * up).astype(bf16)
            hid_ref[pl.ds(base + at, step), :] = hidden
            low = low + dot(v_ref[:, pl.ds(at, step)], hidden, 1, 0)
        base += w_ref.shape[1]

    dp = lax.axis_index("dp")
    here = pl.ds(pl.multiple_of(dp * half, 128), half)
    there = pl.ds(pl.multiple_of((1 - dp) * half, 128), half)
    cross_ref[...] = dot(own_up[...], x_all[:, here], 1, 1) + dot(other_up[...], x_all[:, there], 1, 1)
    lane = lax.broadcasted_iota(jnp.int32, (16, 128), 1)
    row = lax.broadcasted_iota(jnp.int32, (16, 128), 0)
    mine = ((lane & 15) == (own_number() & 15)) & (lane < 48)
    pick = jnp.where(row < 8, mine.astype(f32), (lane == 48).astype(f32)).astype(bf16)
    gates = dot(pick, x_all[:, pl.ds(width, 128)], 1, 1)
    gate_ref[...] = gates
    low_ref[...] = low * gates[0:8]


def send_kernel(low_ref, up_near, sibling_ref, gram_ref, send_ref):
    count = low_ref.shape[1]
    gram_ref[...] = dot(up_near[0:8, :], up_near[...], 1, 1)
    other = dot(sibling_ref[...], up_near[...], 1, 1)
    ordered = dot(low_ref[...].astype(bf16), order_table(count), 1, 1)
    products = jnp.concatenate([gram_ref[...], other], axis=1)
    block = jnp.concatenate([ordered, products], axis=0).astype(bf16)
    for i in range(send_ref.shape[0]):
        send_ref[i] = block


def gradient_kernel(
    near_ref,
    far_ref,
    up_near,
    up_far,
    x_all,
    hid_ref,
    low_ref,
    gram_ref,
    cross_ref,
    gate_ref,
    down_out,
    up_out,
    blocks_buf,
):
    tokens = hid_ref.shape[1]
    blocks = tokens // 4
    half = up_out.shape[1]
    dp = lax.axis_index("dp")
    chip = lax.axis_index("chip")
    chips = lax.axis_size("chip")
    for b in range(blocks):
        away = ((b & 1) << 0) | (((b >> 1) & 1) << 2) | (((b >> 2) & 1) << 1)
        source = far_ref if (b >> 3) & 1 else near_ref
        blocks_buf[b] = source[(dp ^ (b >> 4)) * chips + (chip ^ away)]
    local = dot(blocks_buf[...].reshape(blocks * 16, tokens), order_table(tokens), 1, 0)
    local = local.reshape(2, 16, 16, tokens)[:, :, 0:8]
    lows = (local[0] + local[1]).reshape(tokens, tokens)
    own_low = low_ref[...] + local[1, 0]
    ends = [blocks_buf[b].astype(f32)[8:16] for b in (16, 8, 24)]
    near_rows = up_near.shape[0]
    gram = jnp.concatenate(
        [gram_ref[...] + ends[0][:, :near_rows], ends[1][:, near_rows:] + ends[2][:, near_rows:]], axis=1
    )

    gates = gate_ref[...]
    lane = lax.broadcasted_iota(jnp.int32, (tokens, tokens), 1)
    row = lax.broadcasted_iota(jnp.int32, (tokens, tokens), 0)
    mate = (lane & ~3) | gates[8:9].astype(jnp.int32)
    apart = (row == lane).astype(f32) - (row == mate).astype(f32)
    factors = jnp.concatenate([adapter_scale * lows, -control * apart], axis=0)
    scale = 2.0 / math.sqrt(tokens)

    mixed = dot(own_low, factors, 1, 1, highest_precision)
    high, low = split_two((adapter_scale * scale) * mixed)
    both = jnp.concatenate([high, low], axis=0)
    here = pl.ds(pl.multiple_of(dp * half, 128), half)
    up = (
        dot(both[:, :near_rows], up_near[...], 1, 0)
        + dot(both[:, near_rows:tokens], up_far[...], 1, 0)
        + dot(both[:, tokens:], x_all[:, here], 1, 0)
    )
    up_out[...] = up[0:8] + up[8:16]

    products = jnp.concatenate([gram, cross_ref[...]], axis=1)
    cot_low = dot(products, factors, 1, 0, highest_precision) * gates[0:8]
    high, low = split_two((adapter_scale * scale) * cot_low)
    both = jnp.concatenate([high, low], axis=0)
    down = dot(both, hid_ref[...], 1, 1)
    down_out[...] = down[0:8] + down[8:16]


def dense_body(
    tokens,
    chosen_expert_index,
    router_gate_weight,
    partner,
    gate_up_weight,
    adapter_down_weight,
    adapter_up_weight,
):
    tok_count, width = tokens.shape
    devices = lax.axis_size("dp") * lax.axis_size("chip") * lax.axis_size("core")
    total = tok_count * devices
    units = gate_up_weight.shape[2]
    rank = adapter_up_weight.shape[1]
    half = adapter_up_weight.shape[2]
    vmem = pl.BlockSpec(memory_space=pltpu.VMEM)
    hbm = pl.BlockSpec(memory_space=pltpu.HBM)

    def swap(value, mask):
        return lax.ppermute(value, every, [(i, i ^ mask) for i in range(devices)])

    def grow(value, mask):
        return jnp.concatenate([value, swap(value, mask)], axis=0)

    def stay(value):
        return pltpu.with_memory_space_constraint(value, pltpu.HBM)

    def after(values, other):
        return lax.optimization_barrier((values, other))[0]

    def after(value, other):
        return lax.optimization_barrier((value, other))[0]

    column, own_up = pl.pallas_call(
        start_kernel,
        out_shape=(
            pltpu.VMEM((tok_count, width + 128), bf16),
            pltpu.VMEM((rank, half), bf16),
        ),
        in_specs=[hbm] * 5,
        out_specs=(vmem,) * 2,
        scratch_shapes=[
            pltpu.VMEM(chosen_expert_index.shape, jnp.int32),
            pltpu.VMEM(router_gate_weight.shape, f32),
            pltpu.SMEM(partner.shape, jnp.int32),
            pltpu.SemaphoreType.DMA((5,)),
        ],
        compiler_params=pltpu.CompilerParams(vmem_limit_bytes=2 * mib),
        name="start",
    )(*map(stay, (tokens, adapter_up_weight[0], chosen_expert_index, router_gate_weight, partner)))

    def fetch(first, name, order):
        w, v = after((gate_up_weight[0], adapter_down_weight[0]), order)
        return pl.pallas_call(
            functools.partial(fetch_kernel, first),
            out_shape=(pltpu.VMEM((2, units // 2, width), bf16), pltpu.VMEM((rank, units // 2), bf16)),
            in_specs=[hbm, hbm],
            out_specs=(vmem, vmem),
            scratch_shapes=[pltpu.SemaphoreType.DMA((4,))],
            compiler_params=pltpu.CompilerParams(vmem_limit_bytes=2 * mib),
            cost_estimate=pl.CostEstimate(flops=0, bytes_accessed=8 * mib, transcendentals=0),
            name=name,
        )(stay(w), stay(v))

    weights = fetch(0, "fetch_early", column)
    first = grow(column, 8)
    other_up, sibling, ups = swap(own_up, 16), swap(own_up, 1), swap(own_up, 2)
    first, weights, other_up, sibling, ups = lax.optimization_barrier((first, weights, other_up, sibling, ups))
    late_weights = fetch(units // 2, "fetch_late", first)
    column = grow(first, 4)
    column, late_weights = lax.optimization_barrier((column, late_weights))
    ups = jnp.concatenate([own_up, ups], axis=0)
    third = swap(ups, 8)
    near = [swap(column, 16), swap(column, 2), swap(column, 18)]
    ups = pl.pallas_call(
        join_kernel,
        out_shape=pltpu.VMEM((4 * rank, half), bf16),
        in_specs=[vmem, vmem],
        out_specs=vmem,
        compiler_params=pltpu.CompilerParams(vmem_limit_bytes=2 * mib),
        cost_estimate=pl.CostEstimate(flops=0, bytes_accessed=8 * mib, transcendentals=0),
        name="join",
    )(*after((ups, third), column))
    fourth = swap(ups, 4)
    near = [column] + near
    pieces = near + [swap(piece, 1) for piece in near]

    count = len(pieces)
    hidden, low, cross, gates, everything = pl.pallas_call(
        functools.partial(hidden_kernel, units // 4, count),
        out_shape=(
            pltpu.VMEM((units, total), bf16),
            pltpu.VMEM((rank, total), f32),
            pltpu.VMEM((rank, total), f32),
            pltpu.VMEM((16, total), f32),
            pltpu.VMEM((total, width + 128), bf16),
        ),
        in_specs=[vmem] * (count + 6),
        out_specs=(vmem,) * 5,
        compiler_params=pltpu.CompilerParams(vmem_limit_bytes=8 * mib),
        cost_estimate=pl.CostEstimate(flops=0, bytes_accessed=16 * mib, transcendentals=0),
        name="hidden",
    )(*pieces, *weights, *late_weights, own_up, other_up)

    up_near = jnp.concatenate(after((ups, fourth), low), axis=0)
    up_far = swap(up_near, 1)
    gram, send = pl.pallas_call(
        send_kernel,
        out_shape=(
            jax.ShapeDtypeStruct((rank, total // 2), f32),
            jax.ShapeDtypeStruct((devices // 2, 16, total), bf16),
        ),
        in_specs=[vmem] * 3,
        out_specs=(vmem,) * 2,
        compiler_params=pltpu.CompilerParams(vmem_limit_bytes=4 * mib),
        name="send",
    )(low, up_near, sibling)

    from_near = lax.all_to_all(send, ("dp", "chip"), split_axis=0, concat_axis=0, tiled=True)
    from_far = swap(from_near, 1)

    down, up = pl.pallas_call(
        gradient_kernel,
        out_shape=(
            jax.ShapeDtypeStruct((rank, units), f32),
            jax.ShapeDtypeStruct((rank, half), f32),
        ),
        in_specs=[vmem] * 10,
        out_specs=(vmem, vmem),
        scratch_shapes=[pltpu.VMEM((devices, 16, total), bf16)],
        compiler_params=pltpu.CompilerParams(vmem_limit_bytes=16 * mib),
        name="gradient",
    )(
        from_near, from_far, up_near, up_far, everything, hidden, low, gram, cross, gates
    )
    return (down[None], up[None])


def solution(mesh):
    groups, experts = mesh.shape["dp"], mesh.shape["expert"]
    if (groups, experts) == (2, 16):
        cut = Mesh(mesh.devices.reshape(groups, experts // 2, 2), every)
        data, owners = every, ("chip", "core")
        run, mesh = dense_body, cut
    else:
        data, owners = ("dp", "expert"), "expert"
        run = slot_body
    placed = (
        P(data, None),
        P(data, None),
        P(data, None),
        P(data),
        P(owners, None, "dp", None),
        P(owners, None, "dp"),
        P(owners, None, "dp"),
    )
    return jax.shard_map(
        run,
        mesh=mesh,
        in_specs=placed,
        out_specs=(P(owners, None, "dp"), P(owners, None, "dp")),
        check_vma=False,
    )
```

```python
import functools
import math

import jax
import jax.numpy as jnp
from jax import lax
from jax.experimental import pallas as pl
from jax.experimental.pallas import tpu as pltpu
from jax.sharding import Mesh
from jax.sharding import PartitionSpec as P

adapter_scale = 2.0
control = 0.5
highest_precision = lax.Precision.HIGHEST
f32 = jnp.float32
bf16 = jnp.bfloat16
every = ("dp", "chip", "core")
mib = 1 << 20


def route_tables(chosen_expert_index, router_gate_weight, experts, capacity):
    tok_count, choices = chosen_expert_index.shape
    picks = (chosen_expert_index[:, :, None] == jnp.arange(experts, dtype=jnp.int32)).astype(
        jnp.int32
    )
    flat = picks.reshape(tok_count * choices, experts)
    before = jnp.cumsum(flat, axis=0) - flat
    slots = jnp.sum(before * flat, axis=1).reshape(tok_count, choices)
    places = (slots[:, :, None] == jnp.arange(capacity, dtype=jnp.int32)).astype(jnp.float32)
    chosen = picks.astype(jnp.float32)
    select = jnp.einsum("tke,tkc->ect", chosen, places, precision=highest_precision)
    weighted = jnp.einsum(
        "tke,tkc,tk->ect", chosen, places, router_gate_weight, precision=highest_precision
    )
    return (select.astype(jnp.bfloat16), weighted)


def expert_hidden(rows, w_local):
    flat_rows = rows.reshape(-1, rows.shape[-1])
    both = jnp.einsum("gfd,nd->gfn", w_local, flat_rows, preferred_element_type=jnp.float32)
    return (jax.nn.silu(both[0]) * both[1]).astype(jnp.bfloat16)


def slot_body(
    tokens,
    chosen_expert_index,
    router_gate_weight,
    partner,
    gate_up_weight,
    adapter_down_weight,
    adapter_up_weight,
):
    tok_count, width = tokens.shape
    choices = chosen_expert_index.shape[1]
    groups = lax.axis_size("dp")
    experts = lax.axis_size("expert")
    capacity = min(tok_count, max(2, (2 * tok_count * choices + experts - 1) // experts))
    select, weighted = route_tables(chosen_expert_index, router_gate_weight, experts, capacity)
    w_local = gate_up_weight[0]
    down_factor = adapter_down_weight[0]
    up_factor = adapter_up_weight[0]
    slice_width = up_factor.shape[1]
    outgoing = jnp.einsum("ect,td->ecd", select, tokens, preferred_element_type=jnp.float32).astype(
        jnp.bfloat16
    )
    arrived = lax.all_to_all(outgoing[None], "expert", split_axis=1, concat_axis=1, tiled=True)
    hidden_state = expert_hidden(lax.all_gather(arrived, "dp", axis=0, tiled=True), w_local)
    grid = (groups, experts, capacity)
    partial_low = jnp.einsum(
        "fn,rf->nr", hidden_state, down_factor, preferred_element_type=jnp.float32
    )
    narrow_product = lax.psum(partial_low, "dp")
    delta_flat = (
        adapter_scale
        * jnp.einsum(
            "hy,ya->ha", narrow_product, up_factor.astype(jnp.float32), precision=highest_precision
        )
    ).astype(jnp.bfloat16)
    change_rows = delta_flat.reshape(grid + (slice_width,))
    returned = lax.all_to_all(
        lax.all_to_all(change_rows, "dp", split_axis=0, concat_axis=3, tiled=True),
        "expert",
        split_axis=1,
        concat_axis=1,
        tiled=True,
    )
    returned = returned.reshape(experts, capacity, width)
    delta = jnp.einsum(
        "ect,ecd->td", weighted, returned.astype(jnp.float32), precision=highest_precision
    )
    total = tok_count * groups * experts
    mates = jnp.take(tokens, partner, axis=0).astype(jnp.float32)
    direction = tokens.astype(jnp.float32) - mates
    cotangent = 2.0 / math.sqrt(total) * (delta - control * direction)
    cot_rows = jnp.einsum("ect,td->ecd", weighted, cotangent, precision=highest_precision).astype(
        jnp.bfloat16
    )
    sectioned = cot_rows.reshape(1, experts, capacity, groups, slice_width)
    cot_in = lax.all_to_all(
        lax.all_to_all(sectioned, "dp", split_axis=3, concat_axis=0, tiled=True),
        "expert",
        split_axis=1,
        concat_axis=1,
        tiled=True,
    )
    cot_in = cot_in.reshape(-1, slice_width)
    partial_cot = jnp.einsum("nd,rd->nr", cot_in, up_factor, preferred_element_type=jnp.float32)
    cotangent_narrow = lax.psum(partial_cot, "dp")
    up_factor_gradient = adapter_scale * jnp.einsum(
        "nr,nd->rd", narrow_product, cot_in.astype(jnp.float32), precision=highest_precision
    )
    down_factor_gradient = adapter_scale * jnp.einsum(
        "nr,fn->rf", cotangent_narrow, hidden_state.astype(jnp.float32), precision=highest_precision
    )
    return (down_factor_gradient[None], up_factor_gradient[None])


def mask_of(block):
    return (
        ((block & 1) << 3)
        | (((block >> 1) & 1) << 2)
        | (((block >> 2) & 1) << 4)
        | (((block >> 3) & 1) << 1)
        | ((block >> 4) & 1)
    )


def own_number():
    return (lax.axis_index("dp") * lax.axis_size("chip") + lax.axis_index("chip")) * 2 + (
        lax.axis_index("core")
    )


def dot(left, right, left_dim, right_dim, precision=None):
    return lax.dot_general(
        left,
        right,
        (((left_dim,), (right_dim,)), ((), ())),
        precision=precision,
        preferred_element_type=f32,
    )


def split_two(value):
    high = value.astype(bf16)
    return high, (value - high.astype(f32)).astype(bf16)


def order_table(count):
    lane = lax.broadcasted_iota(jnp.int32, (count, count), 1)
    row = lax.broadcasted_iota(jnp.int32, (count, count), 0)
    whole = ((mask_of(lane >> 2) ^ own_number()) << 2) | (lane & 3)
    return (row == whole).astype(f32).astype(bf16)


def start_kernel(
    x_ref, u_ref, index_ref, gate_ref, partner_ref, out_ref, up_ref, index_v, gate_v, partner_s, sems
):
    count, width = x_ref.shape
    copies = [
        pltpu.make_async_copy(index_ref, index_v, sems.at[0]),
        pltpu.make_async_copy(gate_ref, gate_v, sems.at[1]),
        pltpu.make_async_copy(partner_ref, partner_s, sems.at[2]),
        pltpu.make_async_copy(u_ref, up_ref, sems.at[3]),
        pltpu.make_async_copy(x_ref, out_ref.at[:, pl.ds(0, width)], sems.at[4]),
    ]
    for copy in copies:
        copy.start()
    for copy in copies[:3]:
        copy.wait()
    lane = lax.broadcasted_iota(jnp.int32, (count, 128), 1)
    row = lax.broadcasted_iota(jnp.int32, (count, 128), 0)
    index, gate = index_v[...], gate_v[...]
    dense = jnp.zeros((count, 128), f32)
    for k in range(index.shape[1]):
        dense = dense + jnp.where((lane & 15) == index[:, k : k + 1], gate[:, k : k + 1], 0.0)
    mates = jnp.zeros((count, 128), f32)
    for t in range(count):
        mates = mates + jnp.where((row == t) & (lane == 48), partner_s[t].astype(f32), 0.0)
    high = dense.astype(bf16).astype(f32)
    middle = (dense - high).astype(bf16).astype(f32)
    low = dense - high - middle
    parts = jnp.where(lane < 16, high, jnp.where(lane < 32, middle, jnp.where(lane < 48, low, mates)))
    out_ref[:, pl.ds(width, 128)] = parts.astype(bf16)
    copies[3].wait()
    copies[4].wait()


def fetch_kernel(first, w_ref, v_ref, w_out, v_out, sems):
    units = w_out.shape[1]
    parts = sems.shape[0] - 1
    rows = units // parts
    copies = [pltpu.make_async_copy(v_ref.at[:, pl.ds(first, units)], v_out, sems.at[parts])]
    for i in range(parts):
        copies.append(
            pltpu.make_async_copy(
                w_ref.at[:, pl.ds(first + i * rows, rows), :], w_out.at[:, pl.ds(i * rows, rows), :], sems.at[i]
            )
        )
    for copy in copies:
        copy.start()
    for copy in copies:
        copy.wait()


def join_kernel(first_ref, second_ref, out_ref):
    rows = first_ref.shape[0]
    out_ref[pl.ds(0, rows), :] = first_ref[...]
    out_ref[pl.ds(rows, rows), :] = second_ref[...]


def hidden_kernel(step, pieces, *refs):
    x_refs = refs[:pieces][::-1]
    early_w, early_v, late_w, late_v = refs[pieces : pieces + 4]
    hid_ref, low_ref, gate_ref, x_all = refs[pieces + 4 :]
    at = 0
    for ref in x_refs:
        x_all[pl.ds(at, ref.shape[0]), :] = ref[...]
        at += ref.shape[0]
    width = early_w.shape[2]
    x = x_all[:, pl.ds(0, width)]
    low = jnp.zeros(low_ref.shape, f32)
    base = 0
    for w_ref, v_ref in ((early_w, early_v), (late_w, late_v)):
        for at in range(0, w_ref.shape[1], step):
            gate = dot(w_ref[0, pl.ds(at, step), :], x, 1, 1)
            up = dot(w_ref[1, pl.ds(at, step), :], x, 1, 1)
            hidden = (gate / (1.0 + jnp.exp(-gate)) * up).astype(bf16)
            hid_ref[pl.ds(base + at, step), :] = hidden
            low = low + dot(v_ref[:, pl.ds(at, step)], hidden, 1, 0)
        base += w_ref.shape[1]

    lane = lax.broadcasted_iota(jnp.int32, (16, 128), 1)
    row = lax.broadcasted_iota(jnp.int32, (16, 128), 0)
    mine = ((lane & 15) == (own_number() & 15)) & (lane < 48)
    pick = jnp.where(row < 8, mine.astype(f32), (lane == 48).astype(f32)).astype(bf16)
    gates = dot(pick, x_all[:, pl.ds(width, 128)], 1, 1)
    gate_ref[...] = gates
    low_ref[...] = low * gates[0:8]


def send_kernel(low_ref, up_near, sibling_ref, gram_ref, send_ref):
    count = low_ref.shape[1]
    gram_ref[...] = dot(up_near[0:8, :], up_near[...], 1, 1)
    other = dot(sibling_ref[...], up_near[...], 1, 1)
    ordered = dot(low_ref[...].astype(bf16), order_table(count), 1, 1)
    products = jnp.concatenate([gram_ref[...], other], axis=1)
    block = jnp.concatenate([ordered, products], axis=0).astype(bf16)
    for i in range(send_ref.shape[0]):
        send_ref[i] = block


def table_kernel(x_all, own_up, other_up, gate_ref, cross_ref, factors_ref, order_ref):
    tokens = x_all.shape[0]
    half = own_up.shape[1]
    dp = lax.axis_index("dp")
    here = pl.ds(pl.multiple_of(dp * half, 128), half)
    there = pl.ds(pl.multiple_of((1 - dp) * half, 128), half)
    cross_ref[...] = dot(own_up[...], x_all[:, here], 1, 1) + dot(other_up[...], x_all[:, there], 1, 1)
    lane = lax.broadcasted_iota(jnp.int32, (tokens, tokens), 1)
    row = lax.broadcasted_iota(jnp.int32, (tokens, tokens), 0)
    mate = (lane & ~3) | gate_ref[8:9].astype(jnp.int32)
    factors_ref[...] = control * ((row == mate).astype(f32) - (row == lane).astype(f32)).astype(bf16)
    order_ref[...] = order_table(tokens)


def gradient_kernel(
    near_ref,
    far_ref,
    up_near,
    up_far,
    x_all,
    hid_ref,
    low_ref,
    gram_ref,
    cross_ref,
    gate_ref,
    apart_ref,
    order_ref,
    down_out,
    up_out,
    blocks_buf,
):
    tokens = hid_ref.shape[1]
    blocks = tokens // 4
    half = up_out.shape[1]
    dp = lax.axis_index("dp")
    chip = lax.axis_index("chip")
    chips = lax.axis_size("chip")
    for b in range(blocks):
        away = ((b & 1) << 0) | (((b >> 1) & 1) << 2) | (((b >> 2) & 1) << 1)
        source = far_ref if (b >> 3) & 1 else near_ref
        blocks_buf[b] = source[(dp ^ (b >> 4)) * chips + (chip ^ away)]
    local = dot(blocks_buf[...].reshape(blocks * 16, tokens), order_ref[...], 1, 0)
    local = local.reshape(2, 16, 16, tokens)[:, :, 0:8]
    lows = (local[0] + local[1]).reshape(tokens, tokens)
    own_low = low_ref[...] + local[1, 0]
    ends = [blocks_buf[b].astype(f32)[8:16] for b in (16, 8, 24)]
    near_rows = up_near.shape[0]
    gram = jnp.concatenate(
        [gram_ref[...] + ends[0][:, :near_rows], ends[1][:, near_rows:] + ends[2][:, near_rows:]], axis=1
    )

    scale = 2.0 * adapter_scale / math.sqrt(tokens)
    lows_high, lows_low = split_two(adapter_scale * lows)
    apart = apart_ref[...]

    def three(left, high, low, dim):
        left_high, left_low = split_two(left)
        both = dot(jnp.concatenate([left_high, left_low], axis=0), high, 1, dim)
        return both[0:8] + both[8:16] + dot(left_high, low, 1, dim)

    def two(left, right, dim):
        both = dot(jnp.concatenate(split_two(left), axis=0), right, 1, dim)
        return both[0:8] + both[8:16]

    mixed = scale * three(own_low, lows_high, lows_low, 1)
    mixed_x = scale * two(own_low, apart, 1)
    here = pl.ds(pl.multiple_of(dp * half, 128), half)
    mixed = jnp.concatenate(split_two(mixed), axis=0)
    mixed_x = jnp.concatenate(split_two(mixed_x), axis=0)
    up = (
        dot(mixed[:, :near_rows], up_near[...], 1, 0)
        + dot(mixed[:, near_rows:], up_far[...], 1, 0)
        + dot(mixed_x, x_all[:, here], 1, 0)
    )
    up_out[...] = up[0:8] + up[8:16]

    cot_low = three(gram, lows_high, lows_low, 0) + two(cross_ref[...], apart, 0)
    down_out[...] = two(scale * gate_ref[0:8] * cot_low, hid_ref[...], 1)


def dense_body(
    tokens,
    chosen_expert_index,
    router_gate_weight,
    partner,
    gate_up_weight,
    adapter_down_weight,
    adapter_up_weight,
):
    tok_count, width = tokens.shape
    devices = lax.axis_size("dp") * lax.axis_size("chip") * lax.axis_size("core")
    total = tok_count * devices
    units = gate_up_weight.shape[2]
    rank = adapter_up_weight.shape[1]
    half = adapter_up_weight.shape[2]
    vmem = pl.BlockSpec(memory_space=pltpu.VMEM)
    hbm = pl.BlockSpec(memory_space=pltpu.HBM)

    def swap(value, mask):
        return lax.ppermute(value, every, [(i, i ^ mask) for i in range(devices)])

    def grow(value, mask):
        return jnp.concatenate([value, swap(value, mask)], axis=0)

    def stay(value):
        return pltpu.with_memory_space_constraint(value, pltpu.HBM)

    def after(values, other):
        return lax.optimization_barrier((values, other))[0]

    column, own_up = pl.pallas_call(
        start_kernel,
        out_shape=(
            pltpu.VMEM((tok_count, width + 128), bf16),
            pltpu.VMEM((rank, half), bf16),
        ),
        in_specs=[hbm] * 5,
        out_specs=(vmem,) * 2,
        scratch_shapes=[
            pltpu.VMEM(chosen_expert_index.shape, jnp.int32),
            pltpu.VMEM(router_gate_weight.shape, f32),
            pltpu.SMEM(partner.shape, jnp.int32),
            pltpu.SemaphoreType.DMA((5,)),
        ],
        compiler_params=pltpu.CompilerParams(vmem_limit_bytes=2 * mib),
        name="start",
    )(*map(stay, (tokens, adapter_up_weight[0], chosen_expert_index, router_gate_weight, partner)))

    def fetch(first, name, order):
        w, v = after((gate_up_weight[0], adapter_down_weight[0]), order)
        return pl.pallas_call(
            functools.partial(fetch_kernel, first),
            out_shape=(pltpu.VMEM((2, units // 2, width), bf16), pltpu.VMEM((rank, units // 2), bf16)),
            in_specs=[hbm, hbm],
            out_specs=(vmem, vmem),
            scratch_shapes=[pltpu.SemaphoreType.DMA((4,))],
            compiler_params=pltpu.CompilerParams(vmem_limit_bytes=2 * mib),
            cost_estimate=pl.CostEstimate(flops=0, bytes_accessed=8 * mib, transcendentals=0),
            name=name,
        )(stay(w), stay(v))

    first = grow(column, 8)
    other_up, sibling, ups = swap(own_up, 16), swap(own_up, 1), swap(own_up, 2)
    weights = fetch(0, "fetch_early", first)
    column = grow(first, 4)
    column, weights, other_up, sibling, ups = lax.optimization_barrier((column, weights, other_up, sibling, ups))
    late_weights = fetch(units // 2, "fetch_late", column)
    ups = jnp.concatenate([own_up, ups], axis=0)
    third = swap(ups, 8)
    near = [swap(column, 16), swap(column, 2), swap(column, 18)]
    ups = pl.pallas_call(
        join_kernel,
        out_shape=pltpu.VMEM((4 * rank, half), bf16),
        in_specs=[vmem, vmem],
        out_specs=vmem,
        compiler_params=pltpu.CompilerParams(vmem_limit_bytes=2 * mib),
        cost_estimate=pl.CostEstimate(flops=0, bytes_accessed=8 * mib, transcendentals=0),
        name="join",
    )(*after((ups, third), column))
    fourth = swap(ups, 4)
    near, late_weights = lax.optimization_barrier((near[::-1], late_weights))
    near = near[::-1]
    near = [column] + near
    pieces = near + [swap(piece, 1) for piece in near]

    count = len(pieces)
    hidden, low, gates, everything = pl.pallas_call(
        functools.partial(hidden_kernel, units // 4, count),
        out_shape=(
            pltpu.VMEM((units, total), bf16),
            pltpu.VMEM((rank, total), f32),
            pltpu.VMEM((16, total), f32),
            pltpu.VMEM((total, width + 128), bf16),
        ),
        in_specs=[vmem] * (count + 4),
        out_specs=(vmem,) * 4,
        compiler_params=pltpu.CompilerParams(vmem_limit_bytes=8 * mib),
        cost_estimate=pl.CostEstimate(flops=0, bytes_accessed=16 * mib, transcendentals=0),
        name="hidden",
    )(*pieces[::-1], *weights, *late_weights)

    up_near = jnp.concatenate(after((ups, fourth), low), axis=0)
    up_far = swap(up_near, 1)
    gram, send = pl.pallas_call(
        send_kernel,
        out_shape=(
            jax.ShapeDtypeStruct((rank, total // 2), f32),
            jax.ShapeDtypeStruct((devices // 2, 16, total), bf16),
        ),
        in_specs=[vmem] * 3,
        out_specs=(vmem,) * 2,
        compiler_params=pltpu.CompilerParams(vmem_limit_bytes=4 * mib),
        name="send",
    )(low, up_near, sibling)

    from_near = lax.all_to_all(send, ("dp", "chip"), split_axis=0, concat_axis=0, tiled=True)
    from_far = swap(from_near, 1)

    cross, apart, order = pl.pallas_call(
        table_kernel,
        out_shape=(
            pltpu.VMEM((rank, total), f32),
            pltpu.VMEM((total, total), bf16),
            pltpu.VMEM((total, total), bf16),
        ),
        in_specs=[vmem] * 4,
        out_specs=(vmem,) * 3,
        compiler_params=pltpu.CompilerParams(vmem_limit_bytes=4 * mib),
        cost_estimate=pl.CostEstimate(flops=0, bytes_accessed=4 * mib, transcendentals=0),
        name="table",
    )(everything, own_up, other_up, after(gates, from_near))

    down, up = pl.pallas_call(
        gradient_kernel,
        out_shape=(
            jax.ShapeDtypeStruct((rank, units), f32),
            jax.ShapeDtypeStruct((rank, half), f32),
        ),
        in_specs=[vmem] * 12,
        out_specs=(vmem, vmem),
        scratch_shapes=[pltpu.VMEM((devices, 16, total), bf16)],
        compiler_params=pltpu.CompilerParams(vmem_limit_bytes=16 * mib),
        name="gradient",
    )(
        from_near, from_far, up_near, up_far, everything, hidden, low, gram, cross, gates, apart, order
    )
    return (down[None], up[None])


def solution(mesh):
    groups, experts = mesh.shape["dp"], mesh.shape["expert"]
    if (groups, experts) == (2, 16):
        cut = Mesh(mesh.devices.reshape(groups, experts // 2, 2), every)
        data, owners = every, ("chip", "core")
        run, mesh = dense_body, cut
    else:
        data, owners = ("dp", "expert"), "expert"
        run = slot_body
    placed = (
        P(data, None),
        P(data, None),
        P(data, None),
        P(data),
        P(owners, None, "dp", None),
        P(owners, None, "dp"),
        P(owners, None, "dp"),
    )
    return jax.shard_map(
        run,
        mesh=mesh,
        in_specs=placed,
        out_specs=(P(owners, None, "dp"), P(owners, None, "dp")),
        check_vma=False,
    )
```

```python
import functools
import math

import jax
import jax.numpy as jnp
from jax import lax
from jax.experimental import pallas as pl
from jax.experimental.pallas import tpu as pltpu
from jax.sharding import Mesh
from jax.sharding import PartitionSpec as P

adapter_scale = 2.0
control = 0.5
highest_precision = lax.Precision.HIGHEST
f32 = jnp.float32
bf16 = jnp.bfloat16
every = ("dp", "chip", "core")
mib = 1 << 20


def route_tables(chosen_expert_index, router_gate_weight, experts, capacity):
    tok_count, choices = chosen_expert_index.shape
    picks = (chosen_expert_index[:, :, None] == jnp.arange(experts, dtype=jnp.int32)).astype(
        jnp.int32
    )
    flat = picks.reshape(tok_count * choices, experts)
    before = jnp.cumsum(flat, axis=0) - flat
    slots = jnp.sum(before * flat, axis=1).reshape(tok_count, choices)
    places = (slots[:, :, None] == jnp.arange(capacity, dtype=jnp.int32)).astype(jnp.float32)
    chosen = picks.astype(jnp.float32)
    select = jnp.einsum("tke,tkc->ect", chosen, places, precision=highest_precision)
    weighted = jnp.einsum(
        "tke,tkc,tk->ect", chosen, places, router_gate_weight, precision=highest_precision
    )
    return (select.astype(jnp.bfloat16), weighted)


def expert_hidden(rows, w_local):
    flat_rows = rows.reshape(-1, rows.shape[-1])
    both = jnp.einsum("gfd,nd->gfn", w_local, flat_rows, preferred_element_type=jnp.float32)
    return (jax.nn.silu(both[0]) * both[1]).astype(jnp.bfloat16)


def slot_body(
    tokens,
    chosen_expert_index,
    router_gate_weight,
    partner,
    gate_up_weight,
    adapter_down_weight,
    adapter_up_weight,
):
    tok_count, width = tokens.shape
    choices = chosen_expert_index.shape[1]
    groups = lax.axis_size("dp")
    experts = lax.axis_size("expert")
    capacity = min(tok_count, max(2, (2 * tok_count * choices + experts - 1) // experts))
    select, weighted = route_tables(chosen_expert_index, router_gate_weight, experts, capacity)
    w_local = gate_up_weight[0]
    down_factor = adapter_down_weight[0]
    up_factor = adapter_up_weight[0]
    slice_width = up_factor.shape[1]
    outgoing = jnp.einsum("ect,td->ecd", select, tokens, preferred_element_type=jnp.float32).astype(
        jnp.bfloat16
    )
    arrived = lax.all_to_all(outgoing[None], "expert", split_axis=1, concat_axis=1, tiled=True)
    hidden_state = expert_hidden(lax.all_gather(arrived, "dp", axis=0, tiled=True), w_local)
    grid = (groups, experts, capacity)
    partial_low = jnp.einsum(
        "fn,rf->nr", hidden_state, down_factor, preferred_element_type=jnp.float32
    )
    narrow_product = lax.psum(partial_low, "dp")
    delta_flat = (
        adapter_scale
        * jnp.einsum(
            "hy,ya->ha", narrow_product, up_factor.astype(jnp.float32), precision=highest_precision
        )
    ).astype(jnp.bfloat16)
    change_rows = delta_flat.reshape(grid + (slice_width,))
    returned = lax.all_to_all(
        lax.all_to_all(change_rows, "dp", split_axis=0, concat_axis=3, tiled=True),
        "expert",
        split_axis=1,
        concat_axis=1,
        tiled=True,
    )
    returned = returned.reshape(experts, capacity, width)
    delta = jnp.einsum(
        "ect,ecd->td", weighted, returned.astype(jnp.float32), precision=highest_precision
    )
    total = tok_count * groups * experts
    mates = jnp.take(tokens, partner, axis=0).astype(jnp.float32)
    direction = tokens.astype(jnp.float32) - mates
    cotangent = 2.0 / math.sqrt(total) * (delta - control * direction)
    cot_rows = jnp.einsum("ect,td->ecd", weighted, cotangent, precision=highest_precision).astype(
        jnp.bfloat16
    )
    sectioned = cot_rows.reshape(1, experts, capacity, groups, slice_width)
    cot_in = lax.all_to_all(
        lax.all_to_all(sectioned, "dp", split_axis=3, concat_axis=0, tiled=True),
        "expert",
        split_axis=1,
        concat_axis=1,
        tiled=True,
    )
    cot_in = cot_in.reshape(-1, slice_width)
    partial_cot = jnp.einsum("nd,rd->nr", cot_in, up_factor, preferred_element_type=jnp.float32)
    cotangent_narrow = lax.psum(partial_cot, "dp")
    up_factor_gradient = adapter_scale * jnp.einsum(
        "nr,nd->rd", narrow_product, cot_in.astype(jnp.float32), precision=highest_precision
    )
    down_factor_gradient = adapter_scale * jnp.einsum(
        "nr,fn->rf", cotangent_narrow, hidden_state.astype(jnp.float32), precision=highest_precision
    )
    return (down_factor_gradient[None], up_factor_gradient[None])


def mask_of(block):
    return (
        ((block & 1) << 3)
        | (((block >> 1) & 1) << 2)
        | (((block >> 2) & 1) << 4)
        | (((block >> 3) & 1) << 1)
        | ((block >> 4) & 1)
    )


def own_number():
    return (lax.axis_index("dp") * lax.axis_size("chip") + lax.axis_index("chip")) * 2 + (
        lax.axis_index("core")
    )


def dot(left, right, left_dim, right_dim, precision=None):
    return lax.dot_general(
        left,
        right,
        (((left_dim,), (right_dim,)), ((), ())),
        precision=precision,
        preferred_element_type=f32,
    )


def split_two(value):
    high = value.astype(bf16)
    return high, (value - high.astype(f32)).astype(bf16)


def order_table(count):
    lane = lax.broadcasted_iota(jnp.int32, (count, count), 1)
    row = lax.broadcasted_iota(jnp.int32, (count, count), 0)
    whole = ((mask_of(lane >> 2) ^ own_number()) << 2) | (lane & 3)
    return (row == whole).astype(f32).astype(bf16)


def start_kernel(
    x_ref, u_ref, index_ref, gate_ref, partner_ref, out_ref, up_ref, index_v, gate_v, partner_s, sems
):
    count, width = x_ref.shape
    copies = [
        pltpu.make_async_copy(index_ref, index_v, sems.at[0]),
        pltpu.make_async_copy(gate_ref, gate_v, sems.at[1]),
        pltpu.make_async_copy(partner_ref, partner_s, sems.at[2]),
        pltpu.make_async_copy(u_ref, up_ref, sems.at[3]),
        pltpu.make_async_copy(x_ref, out_ref.at[:, pl.ds(0, width)], sems.at[4]),
    ]
    for copy in copies:
        copy.start()
    for copy in copies[:3]:
        copy.wait()
    lane = lax.broadcasted_iota(jnp.int32, (count, 128), 1)
    row = lax.broadcasted_iota(jnp.int32, (count, 128), 0)
    index, gate = index_v[...], gate_v[...]
    dense = jnp.zeros((count, 128), f32)
    for k in range(index.shape[1]):
        dense = dense + jnp.where((lane & 15) == index[:, k : k + 1], gate[:, k : k + 1], 0.0)
    mates = jnp.zeros((count, 128), f32)
    for t in range(count):
        mates = mates + jnp.where((row == t) & (lane == 48), partner_s[t].astype(f32), 0.0)
    high = dense.astype(bf16).astype(f32)
    middle = (dense - high).astype(bf16).astype(f32)
    low = dense - high - middle
    parts = jnp.where(lane < 16, high, jnp.where(lane < 32, middle, jnp.where(lane < 48, low, mates)))
    out_ref[:, pl.ds(width, 128)] = parts.astype(bf16)
    copies[3].wait()
    copies[4].wait()


def fetch_kernel(first, w_ref, v_ref, w_out, v_out, sems):
    units = w_out.shape[1]
    parts = sems.shape[0] - 1
    rows = units // parts
    copies = [pltpu.make_async_copy(v_ref.at[:, pl.ds(first, units)], v_out, sems.at[parts])]
    for i in range(parts):
        copies.append(
            pltpu.make_async_copy(
                w_ref.at[:, pl.ds(first + i * rows, rows), :], w_out.at[:, pl.ds(i * rows, rows), :], sems.at[i]
            )
        )
    for copy in copies:
        copy.start()
    for copy in copies:
        copy.wait()


def join_kernel(first_ref, second_ref, out_ref):
    rows = first_ref.shape[0]
    out_ref[pl.ds(0, rows), :] = first_ref[...]
    out_ref[pl.ds(rows, rows), :] = second_ref[...]


def hidden_kernel(step, pieces, *refs):
    x_refs = refs[:pieces][::-1]
    early_w, early_v, late_w, late_v = refs[pieces : pieces + 4]
    hid_ref, low_ref, gate_ref, x_all = refs[pieces + 4 :]
    at = 0
    for ref in x_refs:
        x_all[pl.ds(at, ref.shape[0]), :] = ref[...]
        at += ref.shape[0]
    width = early_w.shape[2]
    x = x_all[:, pl.ds(0, width)]
    low = jnp.zeros(low_ref.shape, f32)
    base = 0
    for w_ref, v_ref in ((early_w, early_v), (late_w, late_v)):
        for at in range(0, w_ref.shape[1], step):
            both = dot(w_ref[:, pl.ds(at, step), :].reshape(2 * step, width), x, 1, 1)
            gate, up = both[:step], both[step:]
            hidden = (gate / (1.0 + jnp.exp(-gate)) * up).astype(bf16)
            hid_ref[pl.ds(base + at, step), :] = hidden
            low = low + dot(v_ref[:, pl.ds(at, step)], hidden, 1, 0)
        base += w_ref.shape[1]

    lane = lax.broadcasted_iota(jnp.int32, (16, 128), 1)
    row = lax.broadcasted_iota(jnp.int32, (16, 128), 0)
    mine = ((lane & 15) == (own_number() & 15)) & (lane < 48)
    pick = jnp.where(row < 8, mine.astype(f32), (lane == 48).astype(f32)).astype(bf16)
    gates = dot(pick, x_all[:, pl.ds(width, 128)], 1, 1)
    gate_ref[...] = gates
    low_ref[...] = low * gates[0:8]


def send_kernel(low_ref, up_near, sibling_ref, gram_ref, send_ref):
    count = low_ref.shape[1]
    gram_ref[...] = dot(up_near[0:8, :], up_near[...], 1, 1)
    other = dot(sibling_ref[...], up_near[...], 1, 1)
    ordered = dot(low_ref[...].astype(bf16), order_table(count), 1, 1)
    products = jnp.concatenate([gram_ref[...], other], axis=1)
    block = jnp.concatenate([ordered, products], axis=0).astype(bf16)
    for i in range(send_ref.shape[0]):
        send_ref[i] = block


def table_kernel(x_all, own_up, other_up, gate_ref, cross_ref, factors_ref, order_ref):
    tokens = x_all.shape[0]
    half = own_up.shape[1]
    dp = lax.axis_index("dp")
    here = pl.ds(pl.multiple_of(dp * half, 128), half)
    there = pl.ds(pl.multiple_of((1 - dp) * half, 128), half)
    cross_ref[...] = dot(own_up[...], x_all[:, here], 1, 1) + dot(other_up[...], x_all[:, there], 1, 1)
    lane = lax.broadcasted_iota(jnp.int32, (tokens, tokens), 1)
    row = lax.broadcasted_iota(jnp.int32, (tokens, tokens), 0)
    mate = (lane & ~3) | gate_ref[8:9].astype(jnp.int32)
    factors_ref[...] = control * ((row == mate).astype(f32) - (row == lane).astype(f32)).astype(bf16)
    order_ref[...] = order_table(tokens)


def gradient_kernel(
    near_ref,
    far_ref,
    up_near,
    up_far,
    x_all,
    hid_ref,
    low_ref,
    gram_ref,
    cross_ref,
    gate_ref,
    apart_ref,
    order_ref,
    down_out,
    up_out,
    blocks_buf,
):
    tokens = hid_ref.shape[1]
    blocks = tokens // 4
    half = up_out.shape[1]
    dp = lax.axis_index("dp")
    chip = lax.axis_index("chip")
    chips = lax.axis_size("chip")
    for b in range(blocks):
        away = ((b & 1) << 0) | (((b >> 1) & 1) << 2) | (((b >> 2) & 1) << 1)
        source = far_ref if (b >> 3) & 1 else near_ref
        blocks_buf[b] = source[(dp ^ (b >> 4)) * chips + (chip ^ away)]
    local = dot(blocks_buf[...].reshape(blocks * 16, tokens), order_ref[...], 1, 0)
    local = local.reshape(2, 16, 16, tokens)[:, :, 0:8]
    lows = (local[0] + local[1]).reshape(tokens, tokens)
    own_low = low_ref[...] + local[1, 0]
    ends = [blocks_buf[b].astype(f32)[8:16] for b in (16, 8, 24)]
    near_rows = up_near.shape[0]
    gram = jnp.concatenate(
        [gram_ref[...] + ends[0][:, :near_rows], ends[1][:, near_rows:] + ends[2][:, near_rows:]], axis=1
    )

    scale = 2.0 * adapter_scale / math.sqrt(tokens)
    lows_high, lows_low = split_two(adapter_scale * lows)
    apart = apart_ref[...]

    def three(left, high, low, dim):
        left_high, left_low = split_two(left)
        both = dot(jnp.concatenate([left_high, left_low], axis=0), high, 1, dim)
        return both[0:8] + both[8:16] + dot(left_high, low, 1, dim)

    def two(left, right, dim):
        both = dot(jnp.concatenate(split_two(left), axis=0), right, 1, dim)
        return both[0:8] + both[8:16]

    mixed = scale * three(own_low, lows_high, lows_low, 1)
    mixed_x = scale * two(own_low, apart, 1)
    here = pl.ds(pl.multiple_of(dp * half, 128), half)
    mixed = jnp.concatenate(split_two(mixed), axis=0)
    mixed_x = jnp.concatenate(split_two(mixed_x), axis=0)
    up = (
        dot(mixed[:, :near_rows], up_near[...], 1, 0)
        + dot(mixed[:, near_rows:], up_far[...], 1, 0)
        + dot(mixed_x, x_all[:, here], 1, 0)
    )
    up_out[...] = up[0:8] + up[8:16]

    cot_low = three(gram, lows_high, lows_low, 0) + two(cross_ref[...], apart, 0)
    down_out[...] = two(scale * gate_ref[0:8] * cot_low, hid_ref[...], 1)


def dense_body(
    tokens,
    chosen_expert_index,
    router_gate_weight,
    partner,
    gate_up_weight,
    adapter_down_weight,
    adapter_up_weight,
):
    tok_count, width = tokens.shape
    devices = lax.axis_size("dp") * lax.axis_size("chip") * lax.axis_size("core")
    total = tok_count * devices
    units = gate_up_weight.shape[2]
    rank = adapter_up_weight.shape[1]
    half = adapter_up_weight.shape[2]
    vmem = pl.BlockSpec(memory_space=pltpu.VMEM)
    hbm = pl.BlockSpec(memory_space=pltpu.HBM)

    def swap(value, mask):
        return lax.ppermute(value, every, [(i, i ^ mask) for i in range(devices)])

    def grow(value, mask):
        return jnp.concatenate([value, swap(value, mask)], axis=0)

    def stay(value):
        return pltpu.with_memory_space_constraint(value, pltpu.HBM)

    def after(values, other):
        return lax.optimization_barrier((values, other))[0]

    column, own_up = pl.pallas_call(
        start_kernel,
        out_shape=(
            pltpu.VMEM((tok_count, width + 128), bf16),
            pltpu.VMEM((rank, half), bf16),
        ),
        in_specs=[hbm] * 5,
        out_specs=(vmem,) * 2,
        scratch_shapes=[
            pltpu.VMEM(chosen_expert_index.shape, jnp.int32),
            pltpu.VMEM(router_gate_weight.shape, f32),
            pltpu.SMEM(partner.shape, jnp.int32),
            pltpu.SemaphoreType.DMA((5,)),
        ],
        compiler_params=pltpu.CompilerParams(vmem_limit_bytes=2 * mib),
        name="start",
    )(*map(stay, (tokens, adapter_up_weight[0], chosen_expert_index, router_gate_weight, partner)))

    def fetch(first, name, order):
        w, v = after((gate_up_weight[0], adapter_down_weight[0]), order)
        return pl.pallas_call(
            functools.partial(fetch_kernel, first),
            out_shape=(pltpu.VMEM((2, units // 2, width), bf16), pltpu.VMEM((rank, units // 2), bf16)),
            in_specs=[hbm, hbm],
            out_specs=(vmem, vmem),
            scratch_shapes=[pltpu.SemaphoreType.DMA((4,))],
            compiler_params=pltpu.CompilerParams(vmem_limit_bytes=2 * mib),
            cost_estimate=pl.CostEstimate(flops=0, bytes_accessed=8 * mib, transcendentals=0),
            name=name,
        )(stay(w), stay(v))

    first = grow(column, 8)
    other_up, sibling, ups = swap(own_up, 16), swap(own_up, 1), swap(own_up, 2)
    weights = fetch(0, "fetch_early", first)
    column = grow(first, 4)
    column, weights, other_up, sibling, ups = lax.optimization_barrier((column, weights, other_up, sibling, ups))
    late_weights = fetch(units // 2, "fetch_late", column)
    ups = jnp.concatenate([own_up, ups], axis=0)
    third = swap(ups, 8)
    near = [swap(column, 16), swap(column, 2), swap(column, 18)]
    ups = pl.pallas_call(
        join_kernel,
        out_shape=pltpu.VMEM((4 * rank, half), bf16),
        in_specs=[vmem, vmem],
        out_specs=vmem,
        compiler_params=pltpu.CompilerParams(vmem_limit_bytes=2 * mib),
        cost_estimate=pl.CostEstimate(flops=0, bytes_accessed=8 * mib, transcendentals=0),
        name="join",
    )(*after((ups, third), column))
    fourth = swap(ups, 4)
    near, late_weights = lax.optimization_barrier((near[::-1], late_weights))
    near = near[::-1]
    near = [column] + near
    pieces = near + [swap(piece, 1) for piece in near]

    count = len(pieces)
    hidden, low, gates, everything = pl.pallas_call(
        functools.partial(hidden_kernel, units // 2, count),
        out_shape=(
            pltpu.VMEM((units, total), bf16),
            pltpu.VMEM((rank, total), f32),
            pltpu.VMEM((16, total), f32),
            pltpu.VMEM((total, width + 128), bf16),
        ),
        in_specs=[vmem] * (count + 4),
        out_specs=(vmem,) * 4,
        compiler_params=pltpu.CompilerParams(vmem_limit_bytes=8 * mib),
        cost_estimate=pl.CostEstimate(flops=0, bytes_accessed=16 * mib, transcendentals=0),
        name="hidden",
    )(*pieces[::-1], *weights, *late_weights)

    up_near = jnp.concatenate(after((ups, fourth), low), axis=0)
    up_far = swap(up_near, 1)
    gram, send = pl.pallas_call(
        send_kernel,
        out_shape=(
            jax.ShapeDtypeStruct((rank, total // 2), f32),
            jax.ShapeDtypeStruct((devices // 2, 16, total), bf16),
        ),
        in_specs=[vmem] * 3,
        out_specs=(vmem,) * 2,
        compiler_params=pltpu.CompilerParams(vmem_limit_bytes=4 * mib),
        name="send",
    )(low, up_near, sibling)

    from_near = lax.all_to_all(send, ("dp", "chip"), split_axis=0, concat_axis=0, tiled=True)
    from_far = swap(from_near, 1)

    cross, apart, order = pl.pallas_call(
        table_kernel,
        out_shape=(
            pltpu.VMEM((rank, total), f32),
            pltpu.VMEM((total, total), bf16),
            pltpu.VMEM((total, total), bf16),
        ),
        in_specs=[vmem] * 4,
        out_specs=(vmem,) * 3,
        compiler_params=pltpu.CompilerParams(vmem_limit_bytes=4 * mib),
        cost_estimate=pl.CostEstimate(flops=0, bytes_accessed=4 * mib, transcendentals=0),
        name="table",
    )(everything, own_up, other_up, after(gates, from_near))

    down, up = pl.pallas_call(
        gradient_kernel,
        out_shape=(
            jax.ShapeDtypeStruct((rank, units), f32),
            jax.ShapeDtypeStruct((rank, half), f32),
        ),
        in_specs=[vmem] * 12,
        out_specs=(vmem, vmem),
        scratch_shapes=[pltpu.VMEM((devices, 16, total), bf16)],
        compiler_params=pltpu.CompilerParams(vmem_limit_bytes=16 * mib),
        name="gradient",
    )(
        from_near, from_far, up_near, up_far, everything, hidden, low, gram, cross, gates, apart, order
    )
    return (down[None], up[None])


def solution(mesh):
    groups, experts = mesh.shape["dp"], mesh.shape["expert"]
    if (groups, experts) == (2, 16):
        cut = Mesh(mesh.devices.reshape(groups, experts // 2, 2), every)
        data, owners = every, ("chip", "core")
        run, mesh = dense_body, cut
    else:
        data, owners = ("dp", "expert"), "expert"
        run = slot_body
    placed = (
        P(data, None),
        P(data, None),
        P(data, None),
        P(data),
        P(owners, None, "dp", None),
        P(owners, None, "dp"),
        P(owners, None, "dp"),
    )
    return jax.shard_map(
        run,
        mesh=mesh,
        in_specs=placed,
        out_specs=(P(owners, None, "dp"), P(owners, None, "dp")),
        check_vma=False,
    )
```

```python
import functools
import math

import jax
import jax.numpy as jnp
from jax import lax
from jax.experimental import pallas as pl
from jax.experimental.pallas import tpu as pltpu
from jax.sharding import Mesh
from jax.sharding import PartitionSpec as P

adapter_scale = 2.0
control = 0.5
highest_precision = lax.Precision.HIGHEST
f32 = jnp.float32
bf16 = jnp.bfloat16
every = ("dp", "chip", "core")
mib = 1 << 20


def route_tables(chosen_expert_index, router_gate_weight, experts, capacity):
    tok_count, choices = chosen_expert_index.shape
    picks = (chosen_expert_index[:, :, None] == jnp.arange(experts, dtype=jnp.int32)).astype(
        jnp.int32
    )
    flat = picks.reshape(tok_count * choices, experts)
    before = jnp.cumsum(flat, axis=0) - flat
    slots = jnp.sum(before * flat, axis=1).reshape(tok_count, choices)
    places = (slots[:, :, None] == jnp.arange(capacity, dtype=jnp.int32)).astype(jnp.float32)
    chosen = picks.astype(jnp.float32)
    select = jnp.einsum("tke,tkc->ect", chosen, places, precision=highest_precision)
    weighted = jnp.einsum(
        "tke,tkc,tk->ect", chosen, places, router_gate_weight, precision=highest_precision
    )
    return (select.astype(jnp.bfloat16), weighted)


def expert_hidden(rows, w_local):
    flat_rows = rows.reshape(-1, rows.shape[-1])
    both = jnp.einsum("gfd,nd->gfn", w_local, flat_rows, preferred_element_type=jnp.float32)
    return (jax.nn.silu(both[0]) * both[1]).astype(jnp.bfloat16)


def slot_body(
    tokens,
    chosen_expert_index,
    router_gate_weight,
    partner,
    gate_up_weight,
    adapter_down_weight,
    adapter_up_weight,
):
    tok_count, width = tokens.shape
    choices = chosen_expert_index.shape[1]
    groups = lax.axis_size("dp")
    experts = lax.axis_size("expert")
    capacity = min(tok_count, max(2, (2 * tok_count * choices + experts - 1) // experts))
    select, weighted = route_tables(chosen_expert_index, router_gate_weight, experts, capacity)
    w_local = gate_up_weight[0]
    down_factor = adapter_down_weight[0]
    up_factor = adapter_up_weight[0]
    slice_width = up_factor.shape[1]
    outgoing = jnp.einsum("ect,td->ecd", select, tokens, preferred_element_type=jnp.float32).astype(
        jnp.bfloat16
    )
    arrived = lax.all_to_all(outgoing[None], "expert", split_axis=1, concat_axis=1, tiled=True)
    hidden_state = expert_hidden(lax.all_gather(arrived, "dp", axis=0, tiled=True), w_local)
    grid = (groups, experts, capacity)
    partial_low = jnp.einsum(
        "fn,rf->nr", hidden_state, down_factor, preferred_element_type=jnp.float32
    )
    narrow_product = lax.psum(partial_low, "dp")
    delta_flat = (
        adapter_scale
        * jnp.einsum(
            "hy,ya->ha", narrow_product, up_factor.astype(jnp.float32), precision=highest_precision
        )
    ).astype(jnp.bfloat16)
    change_rows = delta_flat.reshape(grid + (slice_width,))
    returned = lax.all_to_all(
        lax.all_to_all(change_rows, "dp", split_axis=0, concat_axis=3, tiled=True),
        "expert",
        split_axis=1,
        concat_axis=1,
        tiled=True,
    )
    returned = returned.reshape(experts, capacity, width)
    delta = jnp.einsum(
        "ect,ecd->td", weighted, returned.astype(jnp.float32), precision=highest_precision
    )
    total = tok_count * groups * experts
    mates = jnp.take(tokens, partner, axis=0).astype(jnp.float32)
    direction = tokens.astype(jnp.float32) - mates
    cotangent = 2.0 / math.sqrt(total) * (delta - control * direction)
    cot_rows = jnp.einsum("ect,td->ecd", weighted, cotangent, precision=highest_precision).astype(
        jnp.bfloat16
    )
    sectioned = cot_rows.reshape(1, experts, capacity, groups, slice_width)
    cot_in = lax.all_to_all(
        lax.all_to_all(sectioned, "dp", split_axis=3, concat_axis=0, tiled=True),
        "expert",
        split_axis=1,
        concat_axis=1,
        tiled=True,
    )
    cot_in = cot_in.reshape(-1, slice_width)
    partial_cot = jnp.einsum("nd,rd->nr", cot_in, up_factor, preferred_element_type=jnp.float32)
    cotangent_narrow = lax.psum(partial_cot, "dp")
    up_factor_gradient = adapter_scale * jnp.einsum(
        "nr,nd->rd", narrow_product, cot_in.astype(jnp.float32), precision=highest_precision
    )
    down_factor_gradient = adapter_scale * jnp.einsum(
        "nr,fn->rf", cotangent_narrow, hidden_state.astype(jnp.float32), precision=highest_precision
    )
    return (down_factor_gradient[None], up_factor_gradient[None])


def mask_of(block):
    return (
        ((block & 1) << 3)
        | (((block >> 1) & 1) << 2)
        | (((block >> 2) & 1) << 4)
        | (((block >> 3) & 1) << 1)
        | ((block >> 4) & 1)
    )


def own_number():
    return (lax.axis_index("dp") * lax.axis_size("chip") + lax.axis_index("chip")) * 2 + (
        lax.axis_index("core")
    )


def dot(left, right, left_dim, right_dim, precision=None):
    return lax.dot_general(
        left,
        right,
        (((left_dim,), (right_dim,)), ((), ())),
        precision=precision,
        preferred_element_type=f32,
    )


def split_two(value):
    high = value.astype(bf16)
    return high, (value - high.astype(f32)).astype(bf16)


def order_table(count):
    lane = lax.broadcasted_iota(jnp.int32, (count, count), 1)
    row = lax.broadcasted_iota(jnp.int32, (count, count), 0)
    whole = ((mask_of(lane >> 2) ^ own_number()) << 2) | (lane & 3)
    return (row == whole).astype(f32).astype(bf16)


def start_kernel(
    x_ref, u_ref, index_ref, gate_ref, partner_ref, out_ref, up_ref, index_v, gate_v, partner_s, sems
):
    count, width = x_ref.shape
    copies = [
        pltpu.make_async_copy(index_ref, index_v, sems.at[0]),
        pltpu.make_async_copy(gate_ref, gate_v, sems.at[1]),
        pltpu.make_async_copy(partner_ref, partner_s, sems.at[2]),
        pltpu.make_async_copy(u_ref, up_ref, sems.at[3]),
        pltpu.make_async_copy(x_ref, out_ref.at[:, pl.ds(0, width)], sems.at[4]),
    ]
    for copy in copies:
        copy.start()
    for copy in copies[:3]:
        copy.wait()
    lane = lax.broadcasted_iota(jnp.int32, (count, 128), 1)
    row = lax.broadcasted_iota(jnp.int32, (count, 128), 0)
    index, gate = index_v[...], gate_v[...]
    dense = jnp.zeros((count, 128), f32)
    for k in range(index.shape[1]):
        dense = dense + jnp.where((lane & 15) == index[:, k : k + 1], gate[:, k : k + 1], 0.0)
    mates = jnp.zeros((count, 128), f32)
    for t in range(count):
        mates = mates + jnp.where((row == t) & (lane == 48), partner_s[t].astype(f32), 0.0)
    high = dense.astype(bf16).astype(f32)
    middle = (dense - high).astype(bf16).astype(f32)
    low = dense - high - middle
    parts = jnp.where(lane < 16, high, jnp.where(lane < 32, middle, jnp.where(lane < 48, low, mates)))
    out_ref[:, pl.ds(width, 128)] = parts.astype(bf16)
    copies[3].wait()
    copies[4].wait()


def fetch_kernel(first, w_ref, v_ref, w_out, v_out, sems):
    units = w_out.shape[1]
    parts = sems.shape[0] - 1
    rows = units // parts
    copies = [pltpu.make_async_copy(v_ref.at[:, pl.ds(first, units)], v_out, sems.at[parts])]
    for i in range(parts):
        copies.append(
            pltpu.make_async_copy(
                w_ref.at[:, pl.ds(first + i * rows, rows), :], w_out.at[:, pl.ds(i * rows, rows), :], sems.at[i]
            )
        )
    for copy in copies:
        copy.start()
    for copy in copies:
        copy.wait()


def join_kernel(first_ref, second_ref, out_ref):
    rows = first_ref.shape[0]
    out_ref[pl.ds(0, rows), :] = first_ref[...]
    out_ref[pl.ds(rows, rows), :] = second_ref[...]


def hidden_kernel(step, pieces, *refs):
    x_refs = refs[:pieces][::-1]
    early_w, early_v, late_w, late_v = refs[pieces : pieces + 4]
    hid_ref, low_ref, ordered_ref, gate_ref, x_all = refs[pieces + 4 :]
    at = 0
    for ref in x_refs:
        x_all[pl.ds(at, ref.shape[0]), :] = ref[...]
        at += ref.shape[0]
    width = early_w.shape[2]
    x = x_all[:, pl.ds(0, width)]
    low = jnp.zeros(low_ref.shape, f32)
    base = 0
    for w_ref, v_ref in ((early_w, early_v), (late_w, late_v)):
        for at in range(0, w_ref.shape[1], step):
            both = dot(w_ref[:, pl.ds(at, step), :].reshape(2 * step, width), x, 1, 1)
            gate, up = both[:step], both[step:]
            hidden = (gate / (1.0 + jnp.exp(-gate)) * up).astype(bf16)
            hid_ref[pl.ds(base + at, step), :] = hidden
            low = low + dot(v_ref[:, pl.ds(at, step)], hidden, 1, 0)
        base += w_ref.shape[1]

    lane = lax.broadcasted_iota(jnp.int32, (16, 128), 1)
    row = lax.broadcasted_iota(jnp.int32, (16, 128), 0)
    mine = ((lane & 15) == (own_number() & 15)) & (lane < 48)
    pick = jnp.where(row < 8, mine.astype(f32), (lane == 48).astype(f32)).astype(bf16)
    gates = dot(pick, x_all[:, pl.ds(width, 128)], 1, 1)
    gate_ref[...] = gates
    low = low * gates[0:8]
    low_ref[...] = low
    ordered_ref[...] = dot(low.astype(bf16), order_table(x.shape[0]), 1, 1)


def send_kernel(ordered_ref, up_near, sibling_ref, gram_ref, send_ref):
    gram_ref[...] = dot(up_near[0:8, :], up_near[...], 1, 1)
    other = dot(sibling_ref[...], up_near[...], 1, 1)
    products = jnp.concatenate([gram_ref[...], other], axis=1)
    block = jnp.concatenate([ordered_ref[...], products], axis=0).astype(bf16)
    for i in range(send_ref.shape[0]):
        send_ref[i] = block


def table_kernel(x_all, own_up, other_up, gate_ref, cross_ref, factors_ref, order_ref):
    tokens = x_all.shape[0]
    half = own_up.shape[1]
    dp = lax.axis_index("dp")
    here = pl.ds(pl.multiple_of(dp * half, 128), half)
    there = pl.ds(pl.multiple_of((1 - dp) * half, 128), half)
    cross_ref[...] = dot(own_up[...], x_all[:, here], 1, 1) + dot(other_up[...], x_all[:, there], 1, 1)
    lane = lax.broadcasted_iota(jnp.int32, (tokens, tokens), 1)
    row = lax.broadcasted_iota(jnp.int32, (tokens, tokens), 0)
    mate = (lane & ~3) | gate_ref[8:9].astype(jnp.int32)
    factors_ref[...] = control * ((row == mate).astype(f32) - (row == lane).astype(f32)).astype(bf16)
    order_ref[...] = order_table(tokens)


def gradient_kernel(
    near_ref,
    far_ref,
    up_near,
    up_far,
    x_all,
    hid_ref,
    low_ref,
    gram_ref,
    cross_ref,
    gate_ref,
    apart_ref,
    order_ref,
    down_out,
    up_out,
    blocks_buf,
):
    tokens = hid_ref.shape[1]
    blocks = tokens // 4
    half = up_out.shape[1]
    dp = lax.axis_index("dp")
    chip = lax.axis_index("chip")
    chips = lax.axis_size("chip")
    for b in range(blocks):
        away = ((b & 1) << 0) | (((b >> 1) & 1) << 2) | (((b >> 2) & 1) << 1)
        source = far_ref if (b >> 3) & 1 else near_ref
        blocks_buf[b] = source[(dp ^ (b >> 4)) * chips + (chip ^ away)]
    local = dot(blocks_buf[...].reshape(blocks * 16, tokens), order_ref[...], 1, 0)
    local = local.reshape(2, 16, 16, tokens)[:, :, 0:8]
    lows = (local[0] + local[1]).reshape(tokens, tokens)
    own_low = low_ref[...] + local[1, 0]
    ends = [blocks_buf[b].astype(f32)[8:16] for b in (16, 8, 24)]
    near_rows = up_near.shape[0]
    gram = jnp.concatenate(
        [gram_ref[...] + ends[0][:, :near_rows], ends[1][:, near_rows:] + ends[2][:, near_rows:]], axis=1
    )

    scale = 2.0 * adapter_scale / math.sqrt(tokens)
    lows_high, lows_low = split_two(adapter_scale * lows)
    apart = apart_ref[...]

    def three(left, high, low, dim):
        left_high, left_low = split_two(left)
        both = dot(jnp.concatenate([left_high, left_low], axis=0), high, 1, dim)
        return both[0:8] + both[8:16] + dot(left_high, low, 1, dim)

    def two(left, right, dim):
        both = dot(jnp.concatenate(split_two(left), axis=0), right, 1, dim)
        return both[0:8] + both[8:16]

    mixed = scale * three(own_low, lows_high, lows_low, 1)
    mixed_x = scale * two(own_low, apart, 1)
    here = pl.ds(pl.multiple_of(dp * half, 128), half)
    mixed = jnp.concatenate(split_two(mixed), axis=0)
    mixed_x = jnp.concatenate(split_two(mixed_x), axis=0)
    up = (
        dot(mixed[:, :near_rows], up_near[...], 1, 0)
        + dot(mixed[:, near_rows:], up_far[...], 1, 0)
        + dot(mixed_x, x_all[:, here], 1, 0)
    )
    up_out[...] = up[0:8] + up[8:16]

    cot_low = three(gram, lows_high, lows_low, 0) + two(cross_ref[...], apart, 0)
    down_out[...] = two(scale * gate_ref[0:8] * cot_low, hid_ref[...], 1)


def dense_body(
    tokens,
    chosen_expert_index,
    router_gate_weight,
    partner,
    gate_up_weight,
    adapter_down_weight,
    adapter_up_weight,
):
    tok_count, width = tokens.shape
    devices = lax.axis_size("dp") * lax.axis_size("chip") * lax.axis_size("core")
    total = tok_count * devices
    units = gate_up_weight.shape[2]
    rank = adapter_up_weight.shape[1]
    half = adapter_up_weight.shape[2]
    vmem = pl.BlockSpec(memory_space=pltpu.VMEM)
    hbm = pl.BlockSpec(memory_space=pltpu.HBM)

    def swap(value, mask):
        return lax.ppermute(value, every, [(i, i ^ mask) for i in range(devices)])

    def grow(value, mask):
        return jnp.concatenate([value, swap(value, mask)], axis=0)

    def stay(value):
        return pltpu.with_memory_space_constraint(value, pltpu.HBM)

    def after(values, other):
        return lax.optimization_barrier((values, other))[0]

    column, own_up = pl.pallas_call(
        start_kernel,
        out_shape=(
            pltpu.VMEM((tok_count, width + 128), bf16),
            pltpu.VMEM((rank, half), bf16),
        ),
        in_specs=[hbm] * 5,
        out_specs=(vmem,) * 2,
        scratch_shapes=[
            pltpu.VMEM(chosen_expert_index.shape, jnp.int32),
            pltpu.VMEM(router_gate_weight.shape, f32),
            pltpu.SMEM(partner.shape, jnp.int32),
            pltpu.SemaphoreType.DMA((5,)),
        ],
        compiler_params=pltpu.CompilerParams(vmem_limit_bytes=2 * mib),
        name="start",
    )(*map(stay, (tokens, adapter_up_weight[0], chosen_expert_index, router_gate_weight, partner)))

    def fetch(first, name, order):
        w, v = after((gate_up_weight[0], adapter_down_weight[0]), order)
        return pl.pallas_call(
            functools.partial(fetch_kernel, first),
            out_shape=(pltpu.VMEM((2, units // 2, width), bf16), pltpu.VMEM((rank, units // 2), bf16)),
            in_specs=[hbm, hbm],
            out_specs=(vmem, vmem),
            scratch_shapes=[pltpu.SemaphoreType.DMA((4,))],
            compiler_params=pltpu.CompilerParams(vmem_limit_bytes=2 * mib),
            cost_estimate=pl.CostEstimate(flops=0, bytes_accessed=8 * mib, transcendentals=0),
            name=name,
        )(stay(w), stay(v))

    first = grow(column, 8)
    other_up, sibling, ups = swap(own_up, 16), swap(own_up, 1), swap(own_up, 2)
    weights = fetch(0, "fetch_early", first)
    column = grow(first, 4)
    column, weights, other_up, sibling, ups = lax.optimization_barrier((column, weights, other_up, sibling, ups))
    late_weights = fetch(units // 2, "fetch_late", column)
    ups = jnp.concatenate([own_up, ups], axis=0)
    third = swap(ups, 8)
    near = [swap(column, 16), swap(column, 2), swap(column, 18)]
    ups = pl.pallas_call(
        join_kernel,
        out_shape=pltpu.VMEM((4 * rank, half), bf16),
        in_specs=[vmem, vmem],
        out_specs=vmem,
        compiler_params=pltpu.CompilerParams(vmem_limit_bytes=2 * mib),
        cost_estimate=pl.CostEstimate(flops=0, bytes_accessed=8 * mib, transcendentals=0),
        name="join",
    )(*after((ups, third), column))
    fourth = swap(ups, 4)
    near, late_weights = lax.optimization_barrier((near[::-1], late_weights))
    near = near[::-1]
    near = [column] + near
    pieces = near + [swap(piece, 1) for piece in near]

    count = len(pieces)
    hidden, low, ordered, gates, everything = pl.pallas_call(
        functools.partial(hidden_kernel, units // 2, count),
        out_shape=(
            pltpu.VMEM((units, total), bf16),
            pltpu.VMEM((rank, total), f32),
            pltpu.VMEM((rank, total), f32),
            pltpu.VMEM((16, total), f32),
            pltpu.VMEM((total, width + 128), bf16),
        ),
        in_specs=[vmem] * (count + 4),
        out_specs=(vmem,) * 5,
        compiler_params=pltpu.CompilerParams(vmem_limit_bytes=8 * mib),
        cost_estimate=pl.CostEstimate(flops=0, bytes_accessed=16 * mib, transcendentals=0),
        name="hidden",
    )(*pieces[::-1], *weights, *late_weights)

    up_near = jnp.concatenate(after((ups, fourth), low), axis=0)
    up_far = swap(up_near, 1)
    gram, send = pl.pallas_call(
        send_kernel,
        out_shape=(
            jax.ShapeDtypeStruct((rank, total // 2), f32),
            jax.ShapeDtypeStruct((devices // 2, 16, total), bf16),
        ),
        in_specs=[vmem] * 3,
        out_specs=(vmem,) * 2,
        compiler_params=pltpu.CompilerParams(vmem_limit_bytes=4 * mib),
        name="send",
    )(ordered, up_near, sibling)

    from_near = lax.all_to_all(send, ("dp", "chip"), split_axis=0, concat_axis=0, tiled=True)
    from_far = swap(from_near, 1)

    cross, apart, order = pl.pallas_call(
        table_kernel,
        out_shape=(
            pltpu.VMEM((rank, total), f32),
            pltpu.VMEM((total, total), bf16),
            pltpu.VMEM((total, total), bf16),
        ),
        in_specs=[vmem] * 4,
        out_specs=(vmem,) * 3,
        compiler_params=pltpu.CompilerParams(vmem_limit_bytes=4 * mib),
        cost_estimate=pl.CostEstimate(flops=0, bytes_accessed=4 * mib, transcendentals=0),
        name="table",
    )(everything, own_up, other_up, after(gates, from_near))

    down, up = pl.pallas_call(
        gradient_kernel,
        out_shape=(
            jax.ShapeDtypeStruct((rank, units), f32),
            jax.ShapeDtypeStruct((rank, half), f32),
        ),
        in_specs=[vmem] * 12,
        out_specs=(vmem, vmem),
        scratch_shapes=[pltpu.VMEM((devices, 16, total), bf16)],
        compiler_params=pltpu.CompilerParams(vmem_limit_bytes=16 * mib),
        name="gradient",
    )(
        from_near, from_far, up_near, up_far, everything, hidden, low, gram, cross, gates, apart, order
    )
    return (down[None], up[None])


def solution(mesh):
    groups, experts = mesh.shape["dp"], mesh.shape["expert"]
    if (groups, experts) == (2, 16):
        cut = Mesh(mesh.devices.reshape(groups, experts // 2, 2), every)
        data, owners = every, ("chip", "core")
        run, mesh = dense_body, cut
    else:
        data, owners = ("dp", "expert"), "expert"
        run = slot_body
    placed = (
        P(data, None),
        P(data, None),
        P(data, None),
        P(data),
        P(owners, None, "dp", None),
        P(owners, None, "dp"),
        P(owners, None, "dp"),
    )
    return jax.shard_map(
        run,
        mesh=mesh,
        in_specs=placed,
        out_specs=(P(owners, None, "dp"), P(owners, None, "dp")),
        check_vma=False,
    )
```
